256 devices in a mesh: dp: 16 (over z, core), tp: 16 (over x, y).
Axes of the slice: x: 4, y: 4, z: 8, core: 2. Of those that a mesh axis runs over, the one named last changes fastest.
Arguments:
- token_states: bfloat16 [256, 7168], P('dp', 'tp'), may hold values from -12 to 12
- queries: bfloat16 [4, 256, 64, 576], P(None, ('dp', 'tp')), may hold values from -57 to 57
- kv_cache: bfloat16 [256, 4096, 576], P(('dp', 'tp')), may hold values from -6 to 6
- lengths: int32 [256], P(('dp', 'tp')), may hold values from 1 to 4096, 524288 in all
- attn_gain: float32 [7168], P('tp'), may hold values from 0.5 to 1.5
- kv_gain: float32 [512], replicated, may hold values from 0.5 to 1.5
- w_latent: bfloat16 [7168, 576], P('tp'), may hold values from -0.0625 to 0.0625
- w_out: bfloat16 [32768, 7168], P('dp', 'tp'), may hold values from -0.03125 to 0.03125
- mlp_gain: float32 [7168], P('tp'), may hold values from 0.5 to 1.5
- w_gate_up: bfloat16 [2, 7168, 18432], P(None, 'tp', 'dp'), may hold values from -0.0625 to 0.0625
- w_down: bfloat16 [18432, 7168], P('dp', 'tp'), may hold values from -0.046875 to 0.046875
Outputs:
- mixed: bfloat16 [4, 256, 7168], P(None, 'dp', 'tp')
- latents: bfloat16 [4, 256, 576], P(None, ('dp', 'tp'))
The draws below stay inside these ranges and needn't reach their ends.
Inputs may be any that keep to these rules, and one draw needn't show every extreme that they name: `lengths`: some user holds exactly 4096 cached tokens.
All inputs are finite; a program needn't handle non-finite values. No bound on the sum of `lengths` on one device may be relied on, other than what follows from the above.
Results may differ from the reference program's by a relative error of at most 0.03.
Values may be sent and summed in bfloat16 or wider, within the bound.
A program may use at most 64 MiB of HBM per device.

```python
import math
import jax
import jax.numpy as jnp
import numpy as np
from jax import lax

D = 7168
FF = 18432
LAT = 512
H = 64
KV = 576
STEPS = 4
LMAX = 4096
USERS = 256
N_DP = 16
N_TP = 16


def leading_rows(key):
    key_one, key_two = jax.random.split(key, 2)
    row_zero = jnp.clip(jax.random.normal(key_one, (USERS, KV), jnp.float32), -6.0, 6.0)
    jitter = jnp.clip(jax.random.normal(key_two, (USERS, KV), jnp.float32), -6.0, 6.0)
    row_one = jnp.clip(jitter, -6.0, 6.0)
    return (row_zero, row_one)


def feature_ramp(low_scale, high_scale):
    position = jnp.arange(D, dtype=jnp.float32) / D
    return low_scale * (high_scale / low_scale) ** position


def draw_token_states(key, part):
    key = jax.random.fold_in(key, 17)
    ramp = feature_ramp(0.6, 1.9)
    values = jnp.clip(jax.random.normal(key, (USERS, D), jnp.float32), -6.0, 6.0) * ramp
    return values.astype(jnp.bfloat16)


def draw_kv_cache(key, part):
    row_zero, row_one = leading_rows(key)
    key = jax.random.fold_in(key, 5)
    remaining = jnp.clip(jax.random.normal(key, (USERS, LMAX - 2, KV), jnp.float32), -6.0, 6.0)
    return jnp.concatenate([row_zero[:, None, :], row_one[:, None, :], remaining], axis=1).astype(jnp.bfloat16)


def draw_queries(key, part):
    key = jax.random.fold_in(key, 11)
    key_one = jax.random.fold_in(key, 0)
    values = jnp.clip(jax.random.normal(key_one, (STEPS, USERS, H, KV), jnp.float32), -6.0, 6.0)
    return values.astype(jnp.bfloat16)


def steps_of(own_key, dims, cuts, low, top_value):
    loudness, own = 1.0, jax.random.fold_in(own_key, 6)
    for dim, blocks in cuts:
        draws = jnp.exp(jax.random.uniform(jax.random.fold_in(own, dim), (blocks,), jnp.float32, low / len(cuts), top_value / len(cuts)))
        loudness = loudness * jnp.repeat(draws, dims[dim] // blocks).reshape([-1 if axis == dim else 1 for axis in range(len(dims))])
    return loudness


def split_up(number_of, total, limit, skew):
    portions = [(1 << 20) // math.isqrt(rank ** skew) + 1 for rank in range(2, number_of + 1)]
    surplus, given = total - limit - (number_of - 1), [1] * (number_of - 1)
    while surplus > 0:
        movable = [i for i in range(number_of - 1) if given[i] < limit]
        whole, left = sum([portions[i] for i in movable]), surplus
        for i in movable:
            addition = min(limit - given[i], max(1, left * portions[i] // whole), surplus)
            given[i] = given[i] + addition
            surplus = surplus - addition
    return np.array([limit] + given)


def ragged(stream_key, count, total, most, lean):
    if count == 2:
        one = jax.random.randint(stream_key, (), max(1, total - most), min(most, total - 1) + 1)
        return jnp.stack([one, total - one])
    sizes = jnp.asarray(split_up(count, total, most, lean), jnp.int32)
    couples = (count - 1) // 2
    giver, receiver = sizes[1:1 + 2 * couples:2], sizes[2:2 + 2 * couples:2]
    room = jnp.minimum(giver - 1, most - receiver)
    passed = jax.random.randint(jax.random.fold_in(stream_key, 1), (couples,), 0, 1 << 20) % (room + 1)
    sizes = sizes.at[1:1 + 2 * couples:2].set(giver - passed).at[2:2 + 2 * couples:2].set(receiver + passed)
    return sizes[jax.random.permutation(jax.random.fold_in(stream_key, 2), count)]


def noise(rng, dims, scale, most, cuts=(), kind=jnp.bfloat16):
    entries = jax.random.normal(rng, dims, jnp.float32) * scale
    if len(cuts) > 0:
        entries = steps_of(rng, dims, cuts, -0.22, 0.18) * entries
    return jnp.clip(entries, min=-most, max=most).astype(kind)


def setup_inputs(seed: int = 0) -> dict:
    seeds = jax.random.split(jax.random.key(seed), 12)
    return {
        "token_states": draw_token_states(jax.random.fold_in(seeds[11], 71), 0),
        "queries": draw_queries(jax.random.fold_in(seeds[11], 71), 0),
        "kv_cache": draw_kv_cache(jax.random.fold_in(seeds[11], 71), 0),
        "lengths": ragged(seeds[3], USERS, USERS * LMAX // 2, LMAX, 2).astype(jnp.int32),
        "attn_gain": jnp.clip(1.0 + 0.1 * jax.random.normal(seeds[4], (D,), jnp.float32), 0.5, 1.5),
        "kv_gain": jnp.clip(1.0 + 0.1 * jax.random.normal(seeds[5], (LAT,), jnp.float32), 0.5, 1.5),
        "w_latent": noise(seeds[6], (D, KV), D ** -0.5, 0.0625, ((0, 16),)),
        "w_out": noise(seeds[7], (H * LAT, D), (H * LAT) ** -0.5, 0.03125, ((0, 16), (1, 16))),
        "mlp_gain": jnp.clip(1.0 + 0.1 * jax.random.normal(seeds[8], (D,), jnp.float32), 0.5, 1.5),
        "w_gate_up": noise(seeds[9], (2, D, FF), D ** -0.5, 0.0625, ((1, 16), (2, 16))),
        "w_down": noise(seeds[10], (FF, D), FF ** -0.5, 0.046875, ((0, 16), (1, 16))),
    }


norm_eps = 1e-06
score_scale = 192.0 ** (-0.5)

def rotate_pairs(rope_part, positions):
    half_width = rope_part.shape[1] // 2
    frequency = 10000.0 ** (-jnp.arange(half_width, dtype=jnp.float32) / half_width)
    angles = positions.astype(jnp.float32)[:, None] * frequency[None, :]
    cosine = jnp.cos(angles)
    sine_part = jnp.sin(angles)
    front_half = rope_part[:, :half_width]
    back_half = rope_part[:, half_width:]
    return jnp.concatenate([front_half * cosine - back_half * sine_part, front_half * sine_part + back_half * cosine], axis=1)

def finish_latent(raw_latent, inverse, kv_gain, positions):
    lat_width = kv_gain.shape[0]
    scaled_raw = raw_latent * inverse[:, None]
    content = scaled_raw[:, :lat_width]
    content = content * lax.rsqrt(lax.optimization_barrier(jnp.mean(content * content, axis=1, keepdims=True)) + norm_eps) * kv_gain
    return jnp.concatenate([content, rotate_pairs(scaled_raw[:, lat_width:], positions)], axis=1).astype(jnp.bfloat16)

def new_latent(token_rows, attn_gain, kv_gain, w_latent, positions):
    states = token_rows.astype(jnp.float32)
    scaled = (states * attn_gain).astype(jnp.bfloat16)
    raw_latent = jnp.dot(scaled, w_latent, preferred_element_type=jnp.float32)
    inverse = lax.rsqrt(lax.optimization_barrier(jnp.sum(states * states, axis=1)) / D + norm_eps)
    return finish_latent(raw_latent, inverse, kv_gain, positions)

def attend_user(packed):
    query_block, user_keys, fresh_keys, user_length = packed
    query_float = query_block.astype(jnp.float32)
    cached = jnp.einsum('hk,lk->hl', query_float, user_keys.astype(jnp.float32)) * score_scale
    usable = jnp.arange(user_keys.shape[0], dtype=jnp.int32) < user_length
    cached = jnp.where(usable[None, :], cached, -jnp.inf)
    recent = jnp.einsum('hk,jk->hj', query_float, fresh_keys.astype(jnp.float32)) * score_scale
    highest = jnp.maximum(lax.optimization_barrier(jnp.max(cached, axis=1)), lax.optimization_barrier(jnp.max(recent, axis=1)))
    weight_old = jnp.exp(cached - highest[:, None])
    weight_new = jnp.exp(recent - highest[:, None])
    denominator = lax.optimization_barrier(jnp.sum(weight_old, axis=1)) + lax.optimization_barrier(jnp.sum(weight_new, axis=1))
    prob_old = lax.optimization_barrier((weight_old / denominator[:, None]).astype(jnp.bfloat16)).astype(jnp.float32)
    prob_new = lax.optimization_barrier((weight_new / denominator[:, None]).astype(jnp.bfloat16)).astype(jnp.float32)
    mixed_heads = jnp.einsum('hl,lc->hc', prob_old, user_keys[:, :LAT].astype(jnp.float32))
    mixed_heads = mixed_heads + jnp.einsum('hj,jc->hc', prob_new, fresh_keys[:, :LAT].astype(jnp.float32))
    return mixed_heads.astype(jnp.bfloat16).reshape(-1)

def block_sum(left_side, right_side, part_count):
    block_width = left_side.shape[1] // part_count
    running = jnp.zeros((left_side.shape[0], right_side.shape[1]), jnp.float32)
    for block_index in range(part_count):
        lower_edge = block_index * block_width
        product = jnp.dot(left_side[:, lower_edge:lower_edge + block_width], right_side[lower_edge:lower_edge + block_width], preferred_element_type=jnp.float32)
        running = running + lax.optimization_barrier(product.astype(jnp.bfloat16)).astype(jnp.float32)
    return running

def reference(token_states, queries, kv_cache, lengths, attn_gain, kv_gain, w_latent, w_out, mlp_gain, w_gate_up, w_down):
    fresh_list = []
    mixed_steps = []
    latent_steps = []
    token_rows = token_states
    for step_index in range(STEPS):
        latent = new_latent(token_rows, attn_gain, kv_gain, w_latent, lengths + step_index)
        latent_steps.append(latent)
        fresh_list.append(latent)
        fresh_keys = jnp.stack(fresh_list, axis=1)
        head_outputs = lax.map(attend_user, (queries[step_index], kv_cache, fresh_keys, lengths))
        attn_out = block_sum(head_outputs, w_out, N_DP)
        residual = token_rows.astype(jnp.float32) + attn_out
        inverse = lax.rsqrt(lax.optimization_barrier(jnp.sum(residual * residual, axis=1)) / D + norm_eps)
        normed = (residual * inverse[:, None] * mlp_gain).astype(jnp.bfloat16)
        gate = block_sum(normed, w_gate_up[0], N_TP)
        upper = block_sum(normed, w_gate_up[1], N_TP)
        hidden = (jax.nn.silu(gate) * upper).astype(jnp.bfloat16)
        down_out = block_sum(hidden, w_down, N_DP)
        token_rows = (residual + down_out).astype(jnp.bfloat16)
        mixed_steps.append(token_rows)
    return (jnp.stack(mixed_steps, axis=0), jnp.stack(latent_steps, axis=0))
```

```python
import functools

import jax
import jax.numpy as jnp
import numpy as np
from jax import lax
from jax.experimental import pallas as pl
from jax.experimental.pallas import tpu as pltpu
from jax.sharding import PartitionSpec as P

D = 7168
norm_eps = 1e-06
score_scale = 192.0 ** (-0.5)
MESH = pl.DeviceIdType.MESH
F32 = jnp.float32
BF16 = jnp.bfloat16
NT = (((1,), (1,)), ((), ()))


def layer_kernel(
    width,
    x_ref,
    q_ref,
    len_ref,
    ag_ref,
    kg_ref,
    mg_ref,
    freq_ref,
    kv_hbm,
    wl_hbm,
    wo_hbm,
    wgu_hbm,
    wd_hbm,
    out_ref,
    lat_out,
    kv,
    wl,
    wo,
    wgu,
    wd,
    scores,
    peak,
    total,
    old,
    states,
    resid,
    fresh,
    a_rows,
    a_send,
    a_recv,
    h_send,
    h_recv,
    heads,
    y_rows,
    y_send,
    y_recv,
    normed,
    g_send,
    g_recv,
    hidden,
    d_send,
    d_recv,
    load_sem,
    send_sem,
    recv_sem,
):
    n = x_ref.shape[0]
    steps, head_count, key_width = q_ref.shape
    lat = kg_ref.shape[1]
    ff = wd.shape[0]
    slots = kv.shape[0]
    chunks = load_sem.shape[0] - 4
    chunk = slots // chunks
    g = lax.axis_index("dp")
    t = lax.axis_index("tp")

    def load(src, dst, index):
        return pltpu.make_async_copy(src, dst, load_sem.at[index])

    load_wl = load(wl_hbm, wl, 0)
    load_wo = load(wo_hbm, wo, 1)
    load_wgu = load(wgu_hbm, wgu, 2)
    load_wd = load(wd_hbm, wd, 3)

    def load_kv(index):
        rows = pl.ds(pl.multiple_of(index * chunk, chunk), chunk)
        return load(kv_hbm.at[rows], kv.at[rows], 4 + index)

    load_wl.start()

    @pl.loop(0, chunks)
    def _(index):
        load_kv(index).start()

    load_wo.start()
    load_wgu.start()
    load_wd.start()

    barrier = pltpu.get_barrier_semaphore()

    @pl.loop(1, n)
    def _(i):
        pl.semaphore_signal(barrier, inc=1, device_id=(lax.rem(g + i, n), t), device_id_type=MESH)
        pl.semaphore_signal(barrier, inc=1, device_id=(g, lax.rem(t + i, n)), device_id_type=MESH)

    pl.semaphore_wait(barrier, 2 * (n - 1))

    def send_dp(phase, src, dst):
        @pl.loop(1, n)
        def _(i):
            peer = lax.rem(g + i, n)
            pltpu.make_async_remote_copy(
                src_ref=src(peer),
                dst_ref=dst(g),
                send_sem=send_sem.at[phase],
                recv_sem=recv_sem.at[phase],
                device_id=(peer, t),
                device_id_type=MESH,
            ).start()

    def send_tp(phase, src, dst):
        @pl.loop(1, n)
        def _(i):
            peer = lax.rem(t + i, n)
            pltpu.make_async_remote_copy(
                src_ref=src(peer),
                dst_ref=dst(t),
                send_sem=send_sem.at[phase],
                recv_sem=recv_sem.at[phase],
                device_id=(g, peer),
                device_id_type=MESH,
            ).start()

    def await_bytes(sem, ref):
        pltpu.make_async_copy(ref, ref, sem).wait()

    def rows_of(ref, index):
        return ref.at[pl.ds(pl.multiple_of(index * n, n), n)]

    def first_rows(ref):
        return ref.at[pl.ds(0, n * (n - 1))]

    def first_slots(ref):
        return ref.at[pl.ds(0, n - 1)]

    def send_latent():
        xs = states[...]
        scaled = (xs * ag_ref[...]).astype(BF16)
        a_rows[:, :key_width] = jnp.dot(scaled, wl[...], preferred_element_type=F32)
        squares = jnp.sum(xs * xs, axis=1, keepdims=True)
        a_rows[:, lat + 128 :] = jnp.broadcast_to(squares, (n, 128))
        for i in range(n):
            a_send[i] = a_rows[i : i + 1, :]
        a_recv[t] = a_send[t]
        send_tp(0, lambda peer: a_send.at[peer], lambda me: a_recv.at[me])

    a_rows[...] = jnp.zeros_like(a_rows)
    fresh[...] = jnp.zeros_like(fresh)
    states[...] = x_ref[...].astype(F32)
    load_wl.wait()
    send_latent()

    length = len_ref[0]
    queries = q_ref[...].reshape(steps * head_count, key_width)
    peak[...] = jnp.full_like(peak, -jnp.inf)

    @pl.loop(0, chunks)
    def _(index):
        load_kv(index).wait()
        rows = pl.ds(pl.multiple_of(index * chunk, chunk), chunk)
        part = lax.dot_general(queries, kv[rows], NT, preferred_element_type=F32) * score_scale
        place = lax.broadcasted_iota(jnp.int32, (1, chunk), 1) + index * chunk
        part = jnp.where(place < length, part, -jnp.inf)
        scores[:, rows] = part
        highest = peak[...]
        for k in range(0, chunk, 128):
            highest = jnp.maximum(highest, part[:, k : k + 128])
        peak[...] = highest

    top = jnp.max(peak[...], axis=1, keepdims=True)
    peak[...] = jnp.broadcast_to(top, peak.shape)
    total[...] = jnp.zeros_like(total)
    old[...] = jnp.zeros_like(old)

    @pl.loop(0, chunks)
    def _(index):
        rows = pl.ds(pl.multiple_of(index * chunk, chunk), chunk)
        weights = jnp.exp(scores[:, rows] - peak[:, :1])
        running = total[...]
        for k in range(0, chunk, 128):
            running = running + weights[:, k : k + 128]
        total[...] = running
        old[...] += jnp.dot(weights.astype(BF16), kv[rows, :lat], preferred_element_type=F32)

    total[...] = jnp.broadcast_to(jnp.sum(total[...], axis=1, keepdims=True), total.shape)
    load_wo.wait()
    load_wgu.wait()
    load_wd.wait()

    @pl.loop(0, steps)
    def _(s):
        await_bytes(recv_sem.at[0], first_slots(a_recv))
        await_bytes(send_sem.at[0], first_slots(a_send))
        raw = jnp.sum(a_recv[...], axis=0)
        inverse = lax.rsqrt(raw[:, lat + 128 : lat + 129] / width + norm_eps)
        raw = raw * inverse
        content = raw[:, :lat]
        spread = jnp.mean(content * content, axis=1, keepdims=True)
        content = content * lax.rsqrt(spread + norm_eps) * kg_ref[...]
        rope = raw[:, lat : lat + 128]
        half = (key_width - lat) // 2
        lane = lax.broadcasted_iota(jnp.int32, (1, 128), 1)
        angles = (length + s).astype(F32) * freq_ref[...]
        sine = jnp.sin(angles)
        turned = jnp.where(
            lane < half, -pltpu.roll(rope, 128 - half, 1), pltpu.roll(rope, half, 1)
        )
        rope = rope * jnp.cos(angles) + turned * sine
        latent = jnp.concatenate([content, rope], axis=1)[:, :key_width].astype(BF16)
        lat_out[s] = latent
        fresh[pl.ds(s, 1), :] = latent.astype(F32)

        keys = fresh[...].astype(BF16)
        recent = lax.dot_general(q_ref[s], keys, NT, preferred_element_type=F32) * score_scale
        column = lax.broadcasted_iota(jnp.int32, recent.shape, 1)
        recent = jnp.where(column <= s, recent, -jnp.inf)
        own = pl.ds(pl.multiple_of(s * head_count, head_count), head_count)
        top_old = peak[own, :1]
        highest = jnp.maximum(top_old, jnp.max(recent, axis=1, keepdims=True))
        keep = jnp.exp(top_old - highest)
        weight_new = jnp.exp(recent - highest)
        denominator = total[own, :1] * keep + jnp.sum(weight_new, axis=1, keepdims=True)
        prob_new = (weight_new / denominator).astype(BF16)
        joined = old[own, :] * (keep / denominator) + jnp.dot(
            prob_new, keys[:, :lat], preferred_element_type=F32
        )
        per = head_count // n
        for h in range(head_count):
            h_send[h // per, :, (h % per) * lat : (h % per + 1) * lat] = joined[h : h + 1, :]
        h_recv[g] = h_send[g]
        send_dp(1, lambda peer: h_send.at[peer], lambda me: h_recv.at[me])
        await_bytes(recv_sem.at[1], first_slots(h_recv))
        await_bytes(send_sem.at[1], first_slots(h_send))
        own_rows = pl.ds(pl.multiple_of(t * n, n), n)
        heads[own_rows, :] = h_recv[:, 0, :].astype(BF16)
        send_tp(2, lambda peer: rows_of(heads, t), lambda me: rows_of(heads, me))
        await_bytes(recv_sem.at[2], first_rows(heads))
        await_bytes(send_sem.at[2], first_rows(heads))

        attended = jnp.dot(heads[...], wo[...], preferred_element_type=F32)
        share = attended.shape[1]
        for k in range(0, share, 128):
            size = min(128, share - k)
            y_rows[k // 128, :, :size] = attended[:, k : k + size]
        for i in range(n):
            for k in range(0, share, 128):
                size = min(128, share - k)
                picked = y_rows[k // 128, pl.ds(i, n, stride=n), :]
                y_send[i, :, k : k + size] = picked[:, :size].astype(BF16)
        y_recv[g] = y_send[g]
        send_dp(3, lambda peer: y_send.at[peer], lambda me: y_recv.at[me])
        await_bytes(recv_sem.at[3], first_slots(y_recv))
        await_bytes(send_sem.at[3], first_slots(y_send))
        residual = states[...] + jnp.sum(y_recv[...].astype(F32), axis=0)
        resid[...] = residual

        own_rows = pl.ds(pl.multiple_of(g * n, n), n)
        normed[own_rows, :] = (residual * mg_ref[...]).astype(BF16)
        send_dp(4, lambda peer: rows_of(normed, g), lambda me: rows_of(normed, me))
        await_bytes(recv_sem.at[4], first_rows(normed))
        await_bytes(send_sem.at[4], first_rows(normed))
        unscaled = normed[...].astype(F32) / mg_ref[...]
        squares = jnp.sum(unscaled * unscaled, axis=1, keepdims=True)
        coarse = squares.astype(BF16).astype(F32)
        lane = lax.broadcasted_iota(jnp.int32, (n * n, 128), 1)
        g_send[:, 2 * ff :] = jnp.where(lane < 64, coarse, squares - coarse).astype(BF16)
        for k in range(2):
            g_send[:, k * ff : (k + 1) * ff] = jnp.dot(
                normed[...], wgu[k], preferred_element_type=F32
            ).astype(BF16)
        g_recv[t] = g_send[pl.ds(pl.multiple_of(t * n, n), n), :]
        send_tp(5, lambda peer: rows_of(g_send, peer), lambda me: g_recv.at[me])
        await_bytes(recv_sem.at[5], first_slots(g_recv))
        await_bytes(send_sem.at[5], first_rows(g_send))
        gate_up = jnp.sum(g_recv[...].astype(F32), axis=0)
        squares = jnp.sum(gate_up[:, 2 * ff :], axis=1, keepdims=True) / 64
        inverse = lax.rsqrt(squares / width + norm_eps)
        gate = gate_up[:, :ff] * inverse
        up = gate_up[:, ff : 2 * ff] * inverse
        own_rows = pl.ds(pl.multiple_of(t * n, n), n)
        hidden[own_rows, :] = (gate * jax.nn.sigmoid(gate) * up).astype(BF16)
        send_tp(6, lambda peer: rows_of(hidden, t), lambda me: rows_of(hidden, me))
        await_bytes(recv_sem.at[6], first_rows(hidden))
        await_bytes(send_sem.at[6], first_rows(hidden))

        d_send[...] = jnp.dot(hidden[...], wd[...], preferred_element_type=F32).astype(BF16)
        d_recv[g] = d_send[pl.ds(pl.multiple_of(g * n, n), n), :]
        send_dp(7, lambda peer: rows_of(d_send, peer), lambda me: d_recv.at[me])
        await_bytes(recv_sem.at[7], first_slots(d_recv))
        await_bytes(send_sem.at[7], first_rows(d_send))
        mixed = (resid[...] + jnp.sum(d_recv[...].astype(F32), axis=0)).astype(BF16)
        out_ref[s] = mixed
        states[...] = mixed.astype(F32)

        @pl.when(s < steps - 1)
        def _():
            send_latent()


def body(token_states, queries, kv_cache, lengths, attn_gain, kv_gain, w_latent, w_out, mlp_gain, w_gate_up, w_down):
    n, width = token_states.shape
    steps, _, head_count, key_width = queries.shape
    slots = kv_cache.shape[1]
    lat = kv_gain.shape[0]
    ff = w_down.shape[0]
    depth = w_out.shape[0]
    half = (key_width - lat) // 2
    frequency = np.zeros((1, 128), np.float32)
    frequency[0, : 2 * half] = np.tile(10000.0 ** (-np.arange(half) / half), 2)
    chunk = min(512, slots)
    rows = steps * head_count
    vmem = pl.BlockSpec(memory_space=pltpu.VMEM)
    hbm = pl.BlockSpec(memory_space=pl.ANY)
    mixed, latents = pl.pallas_call(
        functools.partial(layer_kernel, float(width * lax.axis_size("tp"))),
        out_shape=(
            jax.ShapeDtypeStruct((steps, n, width), BF16),
            jax.ShapeDtypeStruct((steps, 1, key_width), BF16),
        ),
        in_specs=[vmem, vmem, pl.BlockSpec(memory_space=pltpu.SMEM)] + [vmem] * 4 + [hbm] * 5,
        out_specs=(vmem, vmem),
        scratch_shapes=[
            pltpu.VMEM((slots, key_width), BF16),
            pltpu.VMEM(w_latent.shape, BF16),
            pltpu.VMEM(w_out.shape, BF16),
            pltpu.VMEM(w_gate_up.shape, BF16),
            pltpu.VMEM(w_down.shape, BF16),
            pltpu.VMEM((rows, slots), F32),
            pltpu.VMEM((rows, 128), F32),
            pltpu.VMEM((rows, 128), F32),
            pltpu.VMEM((rows, lat), F32),
            pltpu.VMEM((n, width), F32),
            pltpu.VMEM((n, width), F32),
            pltpu.VMEM((16, key_width), F32),
            pltpu.VMEM((n, lat + 256), F32),
            pltpu.VMEM((n, 1, lat + 256), F32),
            pltpu.VMEM((n, 1, lat + 256), F32),
            pltpu.VMEM((n, 1, depth), F32),
            pltpu.VMEM((n, 1, depth), F32),
            pltpu.VMEM((n * n, depth), BF16),
            pltpu.VMEM((-(-width // 128), n * n, 128), F32),
            pltpu.VMEM((n, n, width), BF16),
            pltpu.VMEM((n, n, width), BF16),
            pltpu.VMEM((n * n, width), BF16),
            pltpu.VMEM((n * n, 2 * ff + 128), BF16),
            pltpu.VMEM((n, n, 2 * ff + 128), BF16),
            pltpu.VMEM((n * n, ff), BF16),
            pltpu.VMEM((n * n, width), BF16),
            pltpu.VMEM((n, n, width), BF16),
            pltpu.SemaphoreType.DMA((4 + slots // chunk,)),
            pltpu.SemaphoreType.DMA((8,)),
            pltpu.SemaphoreType.DMA((8,)),
        ],
        compiler_params=pltpu.CompilerParams(
            collective_id=0, has_side_effects=True, vmem_limit_bytes=48 * 1024 * 1024
        ),
        name="decode_layer",
    )(
        token_states,
        queries.reshape(steps, head_count, key_width),
        lengths,
        attn_gain.reshape(1, -1),
        kv_gain.reshape(1, -1),
        mlp_gain.reshape(1, -1),
        jnp.asarray(frequency),
        kv_cache.reshape(slots, key_width),
        w_latent,
        w_out,
        w_gate_up,
        w_down,
    )
    return mixed, latents


def solution(mesh):
    placed = (
        P("dp", "tp"),
        P(None, ("dp", "tp"), None, None),
        P(("dp", "tp"), None, None),
        P(("dp", "tp")),
        P("tp"),
        P(),
        P("tp", None),
        P("dp", "tp"),
        P("tp"),
        P(None, "tp", "dp"),
        P("dp", "tp"),
    )
    return jax.shard_map(
        body,
        mesh=mesh,
        in_specs=placed,
        out_specs=(P(None, "dp", "tp"), P(None, ("dp", "tp"), None)),
        check_vma=False,
    )
```

```python
import functools

import jax
import jax.numpy as jnp
import numpy as np
from jax import lax
from jax.experimental import pallas as pl
from jax.experimental.pallas import tpu as pltpu
from jax.sharding import PartitionSpec as P

D = 7168
norm_eps = 1e-06
score_scale = 192.0 ** (-0.5)
MESH = pl.DeviceIdType.MESH
F32 = jnp.float32
BF16 = jnp.bfloat16
NT = (((1,), (1,)), ((), ()))


def layer_kernel(
    width,
    x_hbm,
    q_hbm,
    len_ref,
    ag_hbm,
    kg_hbm,
    mg_hbm,
    freq_hbm,
    kv_hbm,
    wl_hbm,
    wo_hbm,
    wgu_hbm,
    wd_hbm,
    out_ref,
    lat_out,
    x_ref,
    q_ref,
    ag_ref,
    kg_ref,
    mg_ref,
    freq_ref,
    kv,
    wl,
    wo,
    wgu,
    wd,
    scores,
    peak,
    total,
    old,
    states,
    resid,
    fresh,
    a_rows,
    a_send,
    a_recv,
    o_send,
    o_recv,
    old_heads,
    b_send,
    b_recv,
    l_all,
    latents,
    heads,
    y_rows,
    y_send,
    y_recv,
    normed,
    gate_send,
    gate_recv,
    gate_mid,
    gate_last,
    up_send,
    up_recv,
    up_mid,
    up_last,
    hidden,
    d_send,
    d_recv,
    load_sem,
    swap_send,
    swap_recv,
    send_sem,
    recv_sem,
    o_sem,
    o_sent,
    p_sem,
    p_sent,
):
    nt = x_ref.shape[0]
    nz = nt // 2
    side = gate_recv.shape[0]
    steps, head_count, key_width = q_ref.shape
    lat = kg_ref.shape[1]
    ff = wd.shape[2]
    share = wd.shape[1]
    slots = kv.shape[1]
    per = head_count // nz
    half_per = per // 2
    chunks = load_sem.shape[0] - 10
    chunk = slots // chunks
    g = lax.axis_index("dp")
    z = g // 2
    c = lax.rem(g, 2)
    t = lax.axis_index("tp")
    xx = t // side
    yy = lax.rem(t, side)
    sibling = (z * 2 + 1 - c, t)

    def z_peer(i):
        peer = lax.rem(z + i, nz)
        return peer, (peer * 2 + c, t)

    def t_peer(i):
        peer = lax.rem(t + i, nt)
        return peer, (g, peer)

    def x_peer(i):
        peer = lax.rem(xx + i, side)
        return peer, (g, peer * side + yy)

    def y_peer(i):
        peer = lax.rem(yy + i, side)
        return peer, (g, xx * side + peer)

    def load(source, target, index):
        return pltpu.make_async_copy(source, target, load_sem.at[index])

    loads = [
        load(x_hbm, x_ref, 0),
        load(ag_hbm, ag_ref, 1),
        load(wl_hbm, wl, 2),
        load(q_hbm, q_ref, 3),
        load(kg_hbm, kg_ref, 4),
        load(freq_hbm, freq_ref, 5),
        load(mg_hbm, mg_ref, 6),
    ]
    for one in loads:
        one.start()

    def load_kv(index):
        place = pl.ds(pl.multiple_of(index * chunk, chunk), chunk)
        return load(kv_hbm.at[:, place], kv.at[:, place], 10 + index)

    @pl.loop(0, chunks)
    def _(index):
        load_kv(index).start()

    own_weights = [
        load(wo_hbm, wo.at[c], 7),
        load(wgu_hbm, wgu.at[c], 8),
        load(wd_hbm, wd.at[c], 9),
    ]
    for one in own_weights:
        one.start()

    barrier = pltpu.get_barrier_semaphore()

    @pl.loop(1, nz)
    def _(i):
        pl.semaphore_signal(barrier, inc=1, device_id=z_peer(i)[1], device_id_type=MESH)

    @pl.loop(1, nt)
    def _(i):
        pl.semaphore_signal(barrier, inc=1, device_id=t_peer(i)[1], device_id_type=MESH)

    pl.semaphore_signal(barrier, inc=1, device_id=sibling, device_id_type=MESH)
    pl.semaphore_wait(barrier, nz + nt - 1)

    def push(source, target, sent, landed, device):
        return pltpu.make_async_remote_copy(
            src_ref=source,
            dst_ref=target,
            send_sem=sent,
            recv_sem=landed,
            device_id=device,
            device_id_type=MESH,
        )

    swaps = [
        push(source, target.at[c], swap_send.at[k], swap_recv.at[k], sibling)
        for k, (source, target) in enumerate(((wo_hbm, wo), (wgu_hbm, wgu), (wd_hbm, wd)))
    ]

    def send(phase, peer_of, count, source, target):
        @pl.loop(1, count)
        def _(i):
            peer, device = peer_of(i)
            push(source(peer), target, send_sem.at[phase], recv_sem.at[phase], device).start()

    def await_bytes(sem, ref):
        pltpu.make_async_copy(ref, ref, sem).wait()

    def block(ref, index):
        return ref.at[pl.ds(pl.multiple_of(index * nt, nt), nt)]

    def first(ref, count):
        return ref.at[pl.ds(0, count)]

    def landed(phase, ref):
        await_bytes(recv_sem.at[phase], ref)

    def sent(phase, ref):
        await_bytes(send_sem.at[phase], ref)

    def send_latent():
        xs = states[...]
        scaled = (xs * ag_ref[...]).astype(BF16)
        a_rows[:, :key_width] = jnp.dot(scaled, wl[...], preferred_element_type=F32)
        squares = jnp.sum(xs * xs, axis=1, keepdims=True)
        a_rows[:, lat + 128 :] = jnp.broadcast_to(squares, (nt, 128))
        for i in range(nt):
            a_send[i] = a_rows[i : i + 1, :]
        a_recv[t] = a_send[t]
        send(0, t_peer, nt, lambda peer: a_send.at[peer], a_recv.at[t])

    a_rows[...] = jnp.zeros_like(a_rows)
    fresh[...] = jnp.zeros_like(fresh)
    latents[...] = jnp.zeros_like(latents)
    for one in loads[:3]:
        one.wait()
    states[...] = x_ref[...].astype(F32)
    send_latent()
    for one in swaps:
        one.start()

    length = len_ref[0]
    for one in loads[3:]:
        one.wait()
    queries = q_ref[...].reshape(steps * head_count, key_width)
    peak[...] = jnp.full_like(peak, -jnp.inf)

    @pl.loop(0, chunks)
    def _(index):
        load_kv(index).wait()
        place = pl.ds(pl.multiple_of(index * chunk, chunk), chunk)
        part = jnp.dot(queries, kv[:, place], preferred_element_type=F32) * score_scale
        column = lax.broadcasted_iota(jnp.int32, (1, chunk), 1) + index * chunk
        part = jnp.where(column < length, part, -jnp.inf)
        scores[:, place] = part
        highest = peak[...]
        for k in range(0, chunk, 128):
            highest = jnp.maximum(highest, part[:, k : k + 128])
        peak[...] = highest

    top = jnp.max(peak[...], axis=1, keepdims=True)
    peak[...] = jnp.broadcast_to(top, peak.shape)
    total[...] = jnp.zeros_like(total)
    old[...] = jnp.zeros_like(old)

    @pl.loop(0, chunks)
    def _(index):
        place = pl.ds(pl.multiple_of(index * chunk, chunk), chunk)
        weights = jnp.exp(scores[:, place] - peak[:, :1])
        running = total[...]
        for k in range(0, chunk, 128):
            running = running + weights[:, k : k + 128]
        total[...] = running
        old[...] += lax.dot_general(
            weights.astype(BF16), kv[:lat, place], NT, preferred_element_type=F32
        )

    total[...] = jnp.broadcast_to(jnp.sum(total[...], axis=1, keepdims=True), total.shape)

    @pl.loop(0, steps)
    def _(s):
        rows = pl.ds(pl.multiple_of(s * head_count, head_count), head_count)
        whole = old[rows, :] / total[rows, :1]
        for h in range(head_count):
            o_send[s, h] = whole[h : h + 1, :]
        mine = pl.ds(z * per, per)
        o_recv[s, :, z] = o_send[s, mine]

        @pl.loop(1, nz)
        def _(i):
            peer, device = z_peer(i)
            theirs = pl.ds(peer * per, per)
            push(
                o_send.at[s, theirs], o_recv.at[s, :, z], o_sent.at[s], o_sem.at[s], device
            ).start()

    def spread_old(s):
        await_bytes(o_sem.at[s], o_send.at[s, pl.ds(0, per * (nz - 1))])
        await_bytes(o_sent.at[s], o_send.at[s, pl.ds(0, per * (nz - 1))])
        for h in range(half_per):
            pair = [o_recv[s, k * half_per + h, :, 0, :] for k in range(2)]
            old_heads[s, t, :, h * lat : (h + 1) * lat] = jnp.concatenate(pair, axis=0).astype(BF16)

        @pl.loop(1, nt)
        def _(i):
            part = old_heads.at[s, t]
            push(part, part, p_sent.at[s], p_sem.at[s], t_peer(i)[1]).start()

    spread_old(0)
    for one in own_weights:
        one.wait()
    for one in swaps:
        one.wait()

    @pl.loop(0, steps)
    def _(s):
        landed(0, first(a_recv, nt - 1))
        sent(0, first(a_send, nt - 1))
        raw = jnp.sum(a_recv[...], axis=0)
        inverse = lax.rsqrt(raw[:, lat + 128 : lat + 129] / width + norm_eps)
        raw = raw * inverse
        content = raw[:, :lat]
        spread = jnp.mean(content * content, axis=1, keepdims=True)
        content = content * lax.rsqrt(spread + norm_eps) * kg_ref[...]
        rope = raw[:, lat : lat + 128]
        half = (key_width - lat) // 2
        lane = lax.broadcasted_iota(jnp.int32, (1, 128), 1)
        angles = (length + s).astype(F32) * freq_ref[...]
        sine = jnp.sin(angles)
        turned = jnp.where(
            lane < half, -pltpu.roll(rope, 128 - half, 1), pltpu.roll(rope, half, 1)
        )
        rope = rope * jnp.cos(angles) + turned * sine
        latent = jnp.concatenate([content, rope], axis=1)[:, :key_width].astype(BF16)
        lat_out[s] = latent
        fresh[pl.ds(s, 1), :] = latent.astype(F32)

        keys = fresh[...].astype(BF16)
        recent = lax.dot_general(q_ref[s], keys, NT, preferred_element_type=F32) * score_scale
        column = lax.broadcasted_iota(jnp.int32, recent.shape, 1)
        recent = jnp.where(column <= s, recent, -jnp.inf)
        own = pl.ds(pl.multiple_of(s * head_count, head_count), head_count)
        top_old = peak[own, :1]
        highest = jnp.maximum(top_old, jnp.max(recent, axis=1, keepdims=True))
        weight_old = total[own, :1] * jnp.exp(top_old - highest)
        weight_new = jnp.exp(recent - highest)
        denominator = weight_old + jnp.sum(weight_new, axis=1, keepdims=True)
        share_new = (weight_new / denominator).astype(BF16).astype(F32)
        column = lax.broadcasted_iota(jnp.int32, (head_count, 128), 1)
        table = jnp.where(column == 0, weight_old / denominator, 0.0)
        for j in range(steps):
            table = jnp.where(column == j + 1, share_new[:, j : j + 1], table)
        table = jnp.concatenate([table, jnp.zeros((128 - head_count, 128), F32)], axis=0).T
        b_send[0, :, :lat] = latent[:, :lat].astype(F32)
        for k in range(steps + 1):
            b_send[0, :, lat + k * 128 : lat + (k + 1) * 128] = table[k : k + 1, :]
        b_recv[z] = b_send[0]
        send(1, z_peer, nz, lambda peer: b_send.at[0], b_recv.at[z])
        landed(1, first(b_recv, nz - 1))
        sent(1, first(b_recv, nz - 1))
        news = b_recv[:, 0, :]
        lane = lax.broadcasted_iota(jnp.int32, (nz, 128), 1)
        coarse = jnp.zeros((nz, 128), F32)
        for k in range(steps + 1):
            moved = pltpu.roll(
                news[:, lat + k * 128 : lat + (k + 1) * 128],
                lax.rem(k * per - z * per + 128, 128),
                1,
            )
            coarse = jnp.where((lane >= k * per) & (lane < (k + 1) * per), moved, coarse)
        fine = coarse - coarse.astype(BF16).astype(F32)
        upper = jnp.concatenate([news[:, : lat // 2], coarse], axis=1)
        lower = jnp.concatenate([news[:, lat // 2 : lat], fine], axis=1)
        l_all[t] = jnp.concatenate([upper, lower], axis=0).astype(BF16)
        send(2, t_peer, nt, lambda peer: l_all.at[t], l_all.at[t])
        await_bytes(p_sem.at[s], old_heads.at[s, pl.ds(0, nt - 1)])
        await_bytes(p_sent.at[s], old_heads.at[s, pl.ds(0, nt - 1)])
        landed(2, first(l_all, nt - 1))
        sent(2, first(l_all, nt - 1))

        news = l_all[...].astype(F32)
        upper = news[:, :nz, :].reshape(nt * nz, -1)
        lower = news[:, nz:, :].reshape(nt * nz, -1)
        latents[s] = jnp.concatenate([upper[:, : lat // 2], lower[:, : lat // 2]], axis=1)
        table = upper[:, lat // 2 :] + lower[:, lat // 2 :]
        for h in range(half_per):
            pair = old_heads[s, :, :, h * lat : (h + 1) * lat].astype(F32)
            for k in range(2):
                number = k * half_per + h
                joined = pair[:, k * nz : (k + 1) * nz, :].reshape(nt * nz, lat)
                joined = joined * table[:, number : number + 1]
                for j in range(steps):
                    at = (j + 1) * per + number
                    joined = joined + latents[j] * table[:, at : at + 1]
                heads[k, :, h * lat : (h + 1) * lat] = joined.astype(BF16)

        attended = sum(
            lax.dot_general(heads[k], wo[k], NT, preferred_element_type=F32) for k in range(2)
        )
        for k in range(0, share, 128):
            size = min(128, share - k)
            y_rows[k // 128, :, :size] = attended[:, k : k + size]
        for i in range(nz):
            for k in range(0, share, 128):
                size = min(128, share - k)
                picked = y_rows[k // 128, pl.ds(i, nt, stride=nz), :]
                y_send[i, :, k : k + size] = picked[:, :size].astype(BF16)
        y_recv[z] = y_send[z]
        send(3, z_peer, nz, lambda peer: y_send.at[peer], y_recv.at[z])

        @pl.when(s < steps - 1)
        def _():
            spread_old(s + 1)

        landed(3, first(y_recv, nz - 1))
        sent(3, first(y_send, nz - 1))
        residual = states[...] + jnp.sum(y_recv[...].astype(F32), axis=0)
        resid[...] = residual

        block(normed, z)[...] = (residual * mg_ref[...]).astype(BF16)
        send(4, z_peer, nz, lambda peer: block(normed, z), block(normed, z))
        landed(4, first(normed, nt * (nz - 1)))
        sent(4, first(normed, nt * (nz - 1)))

        rows = normed[...]
        for k in range(2):
            gate = jnp.dot(rows, wgu[k, 0], preferred_element_type=F32).astype(BF16)
            for i in range(nz):
                place = 2 * i + k
                gate_send[place // side, place % side, :, :ff] = gate[i * nt : (i + 1) * nt, :]
        unscaled = rows.astype(F32) / mg_ref[...]
        squares = jnp.sum(unscaled * unscaled, axis=1, keepdims=True)
        coarse = squares.astype(BF16).astype(F32)
        lane = lax.broadcasted_iota(jnp.int32, (nt * nz, 128), 1)
        parts = jnp.where(lane < 64, coarse, squares - coarse).astype(BF16)
        for i in range(nt):
            here = i // 2 * nt
            gate_send[i // side, i % side, :, ff:] = parts[here : here + nt, :]
        gate_recv[xx] = gate_send[xx]
        send(5, x_peer, side, lambda peer: gate_send.at[peer], gate_recv.at[xx])
        for k in range(2):
            up = jnp.dot(rows, wgu[k, 1], preferred_element_type=F32).astype(BF16)
            for i in range(nz):
                place = 2 * i + k
                up_send[place % side, place // side] = up[i * nt : (i + 1) * nt, :]
        up_recv[yy] = up_send[yy]
        send(6, y_peer, side, lambda peer: up_send.at[peer], up_recv.at[yy])
        landed(5, first(gate_recv, side - 1))
        for i in range(side):
            gate_mid[i] = jnp.sum(gate_recv[:, i].astype(F32), axis=0).astype(BF16)
        gate_last[yy] = gate_mid[yy]
        send(7, y_peer, side, lambda peer: gate_mid.at[peer], gate_last.at[yy])
        landed(6, first(up_recv, side - 1))
        for i in range(side):
            up_mid[i] = jnp.sum(up_recv[:, i].astype(F32), axis=0).astype(BF16)
        up_last[xx] = up_mid[xx]
        send(8, x_peer, side, lambda peer: up_mid.at[peer], up_last.at[xx])
        sent(5, first(gate_send, side - 1))
        sent(6, first(up_send, side - 1))
        landed(7, first(gate_last, side - 1))
        gate = jnp.sum(gate_last[...].astype(F32), axis=0)
        squares = jnp.sum(gate[:, ff:], axis=1, keepdims=True) / 64
        inverse = lax.rsqrt(squares / width + norm_eps)
        gate = gate[:, :ff] * inverse
        gate = gate * jax.nn.sigmoid(gate) * inverse
        landed(8, first(up_last, side - 1))
        up = jnp.sum(up_last[...].astype(F32), axis=0)
        place = lax.rem(t, 2) * nz + t // 2
        block(hidden, place)[...] = (gate * up).astype(BF16)
        send(9, t_peer, nt, lambda peer: block(hidden, place), block(hidden, place))
        sent(7, first(gate_mid, side - 1))
        sent(8, first(up_mid, side - 1))
        landed(9, first(hidden, nt * (nt - 1)))
        sent(9, first(hidden, nt * (nt - 1)))

        down = sum(
            lax.dot_general(
                hidden[k * nz * nt : (k + 1) * nz * nt, :], wd[k], NT, preferred_element_type=F32
            )
            for k in range(2)
        )
        d_send[...] = down.astype(BF16)
        d_recv[z] = block(d_send, z)[...]
        send(10, z_peer, nz, lambda peer: block(d_send, peer), d_recv.at[z])
        landed(10, first(d_recv, nz - 1))
        sent(10, first(d_recv, nz - 1))
        mixed = (resid[...] + jnp.sum(d_recv[...].astype(F32), axis=0)).astype(BF16)
        out_ref[s] = mixed
        states[...] = mixed.astype(F32)

        @pl.when(s < steps - 1)
        def _():
            send_latent()


def body(token_states, queries, kv_cache, lengths, attn_gain, kv_gain, w_latent, w_out, mlp_gain, w_gate_up, w_down):
    nt, width = token_states.shape
    nz = nt // 2
    side = int(round(nt**0.5))
    steps, _, head_count, key_width = queries.shape
    slots = kv_cache.shape[1]
    lat = kv_gain.shape[0]
    ff = w_down.shape[0]
    depth = w_out.shape[0]
    per = head_count // nz
    half = (key_width - lat) // 2
    frequency = np.zeros((1, 128), np.float32)
    frequency[0, : 2 * half] = np.tile(10000.0 ** (-np.arange(half) / half), 2)
    chunk = min(512, slots)
    rows = steps * head_count
    vmem = pl.BlockSpec(memory_space=pltpu.VMEM)
    hbm = pl.BlockSpec(memory_space=pl.ANY)
    news = lat + (steps + 1) * 128
    block = lat // 2 + 128
    mixed, latents = pl.pallas_call(
        functools.partial(layer_kernel, float(width * lax.axis_size("tp"))),
        out_shape=(
            jax.ShapeDtypeStruct((steps, nt, width), BF16),
            jax.ShapeDtypeStruct((steps, 1, key_width), BF16),
        ),
        in_specs=[hbm, hbm, pl.BlockSpec(memory_space=pltpu.SMEM)] + [hbm] * 9,
        out_specs=(vmem, vmem),
        scratch_shapes=[
            pltpu.VMEM((nt, width), BF16),
            pltpu.VMEM((steps, head_count, key_width), BF16),
            pltpu.VMEM((1, width), F32),
            pltpu.VMEM((1, lat), F32),
            pltpu.VMEM((1, width), F32),
            pltpu.VMEM((1, 128), F32),
            pltpu.VMEM((key_width, slots), BF16),
            pltpu.VMEM(w_latent.shape, BF16),
            pltpu.VMEM((2, width, depth), BF16),
            pltpu.VMEM((2,) + w_gate_up.shape, BF16),
            pltpu.VMEM((2, width, ff), BF16),
            pltpu.VMEM((rows, slots), F32),
            pltpu.VMEM((rows, 128), F32),
            pltpu.VMEM((rows, 128), F32),
            pltpu.VMEM((rows, lat), F32),
            pltpu.VMEM((nt, width), F32),
            pltpu.VMEM((nt, width), F32),
            pltpu.VMEM((16, key_width), F32),
            pltpu.VMEM((nt, lat + 256), F32),
            pltpu.VMEM((nt, 1, lat + 256), F32),
            pltpu.VMEM((nt, 1, lat + 256), F32),
            pltpu.VMEM((steps, head_count, 1, lat), F32),
            pltpu.VMEM((steps, per, nz, 1, lat), F32),
            pltpu.VMEM((steps, nt, 2 * nz, per // 2 * lat), BF16),
            pltpu.VMEM((1, 1, news), F32),
            pltpu.VMEM((nz, 1, news), F32),
            pltpu.VMEM((nt, 2 * nz, block), BF16),
            pltpu.VMEM((steps, nt * nz, lat), F32),
            pltpu.VMEM((2, nt * nz, depth), BF16),
            pltpu.VMEM((-(-width // 128), nt * nz, 128), F32),
            pltpu.VMEM((nz, nt, width), BF16),
            pltpu.VMEM((nz, nt, width), BF16),
            pltpu.VMEM((nz * nt, width), BF16),
            pltpu.VMEM((side, side, nt, ff + 128), BF16),
            pltpu.VMEM((side, side, nt, ff + 128), BF16),
            pltpu.VMEM((side, nt, ff + 128), BF16),
            pltpu.VMEM((side, nt, ff + 128), BF16),
            pltpu.VMEM((side, side, nt, ff), BF16),
            pltpu.VMEM((side, side, nt, ff), BF16),
            pltpu.VMEM((side, nt, ff), BF16),
            pltpu.VMEM((side, nt, ff), BF16),
            pltpu.VMEM((nt * nt, ff), BF16),
            pltpu.VMEM((nz * nt, width), BF16),
            pltpu.VMEM((nz, nt, width), BF16),
            pltpu.SemaphoreType.DMA((10 + slots // chunk,)),
            pltpu.SemaphoreType.DMA((3,)),
            pltpu.SemaphoreType.DMA((3,)),
            pltpu.SemaphoreType.DMA((11,)),
            pltpu.SemaphoreType.DMA((11,)),
            pltpu.SemaphoreType.DMA((steps,)),
            pltpu.SemaphoreType.DMA((steps,)),
            pltpu.SemaphoreType.DMA((steps,)),
            pltpu.SemaphoreType.DMA((steps,)),
        ],
        compiler_params=pltpu.CompilerParams(
            collective_id=0, has_side_effects=True, vmem_limit_bytes=56 * 1024 * 1024
        ),
        name="decode_layer",
    )(
        token_states,
        queries.reshape(steps, head_count, key_width),
        lengths,
        attn_gain.reshape(1, -1),
        kv_gain.reshape(1, -1),
        mlp_gain.reshape(1, -1),
        jnp.asarray(frequency),
        kv_cache.reshape(slots, key_width).T,
        w_latent,
        w_out.T,
        w_gate_up,
        w_down.T,
    )
    return mixed, latents


def solution(mesh):
    placed = (
        P("dp", "tp"),
        P(None, ("dp", "tp"), None, None),
        P(("dp", "tp"), None, None),
        P(("dp", "tp")),
        P("tp"),
        P(),
        P("tp", None),
        P("dp", "tp"),
        P("tp"),
        P(None, "tp", "dp"),
        P("dp", "tp"),
    )
    return jax.shard_map(
        body,
        mesh=mesh,
        in_specs=placed,
        out_specs=(P(None, "dp", "tp"), P(None, ("dp", "tp"), None)),
        check_vma=False,
    )
```

```python
import functools

import jax
import jax.numpy as jnp
import numpy as np
from jax import lax
from jax.experimental import pallas as pl
from jax.experimental.pallas import tpu as pltpu
from jax.sharding import PartitionSpec as P

D = 7168
norm_eps = 1e-06
score_scale = 192.0 ** (-0.5)
MESH = pl.DeviceIdType.MESH
F32 = jnp.float32
BF16 = jnp.bfloat16
NT = (((1,), (1,)), ((), ()))


def layer_kernel(
    width,
    x_hbm,
    q_hbm,
    len_ref,
    ag_hbm,
    kg_hbm,
    mg_hbm,
    freq_hbm,
    kv_hbm,
    wl_hbm,
    wo_hbm,
    wgu_hbm,
    wd_hbm,
    out_ref,
    lat_out,
    x_ref,
    q_ref,
    ag_ref,
    kg_ref,
    mg_ref,
    freq_ref,
    kv,
    wl,
    wo,
    wgu,
    wd,
    wo_rows,
    wd_rows,
    turns,
    mg_inv,
    scores,
    peak,
    total,
    old,
    states,
    resid,
    fresh,
    a_rows,
    a_send,
    a_recv,
    o_send,
    o_recv,
    old_heads,
    b_send,
    b_recv,
    l_all,
    latents,
    heads,
    y_rows,
    y_send,
    y_recv,
    normed,
    gate_send,
    gate_recv,
    gate_mid,
    gate_last,
    up_send,
    up_recv,
    up_mid,
    up_last,
    hidden,
    d_send,
    d_recv,
    load_sem,
    swap_send,
    swap_recv,
    send_sem,
    recv_sem,
    o_sem,
    o_sent,
    p_sem,
    p_sent,
    q_sem,
):
    nt = x_ref.shape[0]
    nz = nt // 2
    side = gate_recv.shape[0]
    steps, head_count, key_width = q_ref.shape
    lat = kg_ref.shape[1]
    ff = wd.shape[2]
    share = wd.shape[1]
    slots = kv.shape[1]
    per = head_count // nz
    half_per = per // 2
    cut = ff // 256 * 128
    middle = (share + 255) // 256 * 128
    parts = ((0, middle), (middle, share)) if middle < share else ((0, share),)
    chunks = load_sem.shape[0] - 10
    chunk = slots // chunks
    g = lax.axis_index("dp")
    z = g // 2
    c = lax.rem(g, 2)
    t = lax.axis_index("tp")
    xx = t // side
    yy = lax.rem(t, side)
    sibling = (z * 2 + 1 - c, t)

    def away(k, count):
        odd = lax.rem(k, 2)
        return count // 2 + k // 2 * (1 - odd) - (k + 1) // 2 * odd

    def z_peer(k):
        peer = lax.rem(z + away(k, nz), nz)
        return peer, (peer * 2 + c, t)

    def t_peer(k):
        px = lax.rem(xx + away(k // side, side), side)
        py = lax.rem(yy + away(lax.rem(k, side), side), side)
        peer = px * side + py
        return peer, (g, peer)

    def x_peer(k):
        peer = lax.rem(xx + away(k, side), side)
        return peer, (g, peer * side + yy)

    def y_peer(k):
        peer = lax.rem(yy + away(k, side), side)
        return peer, (g, xx * side + peer)

    def load(source, target, index):
        return pltpu.make_async_copy(source, target, load_sem.at[index])

    loads = [
        load(x_hbm, x_ref, 0),
        load(ag_hbm, ag_ref, 1),
        load(wl_hbm, wl, 2),
        load(q_hbm, q_ref, 3),
        load(kg_hbm, kg_ref, 4),
        load(freq_hbm, freq_ref, 5),
        load(mg_hbm, mg_ref, 6),
    ]
    for one in loads:
        one.start()

    def load_kv(index):
        place = pl.ds(pl.multiple_of(index * chunk, chunk), chunk)
        return load(kv_hbm.at[:, place], kv.at[:, place], 10 + index)

    @pl.loop(0, chunks)
    def _(index):
        load_kv(index).start()

    own_weights = [
        load(wo_hbm, wo.at[c], 7),
        load(wgu_hbm, wgu.at[c], 8),
        load(wd_hbm, wd.at[c], 9),
    ]
    for one in own_weights:
        one.start()

    barrier = pltpu.get_barrier_semaphore()

    @pl.loop(0, nz - 1)
    def _(i):
        pl.semaphore_signal(barrier, inc=1, device_id=z_peer(i)[1], device_id_type=MESH)

    @pl.loop(0, nt - 1)
    def _(i):
        pl.semaphore_signal(barrier, inc=1, device_id=t_peer(i)[1], device_id_type=MESH)

    pl.semaphore_signal(barrier, inc=1, device_id=sibling, device_id_type=MESH)
    pl.semaphore_wait(barrier, nz + nt - 1)

    def push(source, target, sent, landed, device):
        return pltpu.make_async_remote_copy(
            src_ref=source,
            dst_ref=target,
            send_sem=sent,
            recv_sem=landed,
            device_id=device,
            device_id_type=MESH,
        )

    swaps = [
        push(source, target.at[c], swap_send.at[k], swap_recv.at[k], sibling)
        for k, (source, target) in enumerate(((wo_hbm, wo), (wgu_hbm, wgu), (wd_hbm, wd)))
    ]

    def send(phase, peer_of, count, source, target):
        @pl.loop(0, count - 1)
        def _(i):
            peer, device = peer_of(i)
            push(source(peer), target, send_sem.at[phase], recv_sem.at[phase], device).start()

    def await_bytes(sem, ref):
        pltpu.make_async_copy(ref, ref, sem).wait()

    def block(ref, index):
        return ref.at[pl.ds(pl.multiple_of(index * nt, nt), nt)]

    def first(ref, count):
        return ref.at[pl.ds(0, count)]

    def landed(phase, ref):
        await_bytes(recv_sem.at[phase], ref)

    def sent(phase, ref):
        await_bytes(send_sem.at[phase], ref)

    def send_latent():
        xs = states[...]
        scaled = (xs * ag_ref[...]).astype(BF16)
        a_rows[:, :key_width] = jnp.dot(scaled, wl[...], preferred_element_type=F32)
        squares = jnp.sum(xs * xs, axis=1, keepdims=True)
        a_rows[:, lat + 128 :] = jnp.broadcast_to(squares, (nt, 128))
        for i in range(nt):
            a_send[i] = a_rows[i : i + 1, :]
        a_recv[t] = a_send[t]
        send(0, t_peer, nt, lambda peer: a_send.at[peer], a_recv.at[t])

    a_rows[...] = jnp.zeros_like(a_rows)
    fresh[...] = jnp.zeros_like(fresh)
    latents[...] = jnp.zeros_like(latents)
    for one in loads[:3]:
        one.wait()
    states[...] = x_ref[...].astype(F32)
    send_latent()
    for one in swaps:
        one.start()

    length = len_ref[0]
    for one in loads[3:]:
        one.wait()
    row = lax.broadcasted_iota(jnp.int32, turns.shape[1:], 0)
    angles = (row + length).astype(F32) * freq_ref[...]
    turns[0] = jnp.cos(angles)
    turns[1] = jnp.sin(angles)
    mg_inv[...] = 1.0 / mg_ref[...]

    def attend(low, high, arriving):
        rows = pl.ds(low * head_count, (high - low) * head_count)
        queries = q_ref[low:high].reshape((high - low) * head_count, key_width)
        peak[rows, :] = jnp.full((rows.size, 128), -jnp.inf, F32)

        @pl.loop(0, chunks)
        def _(index):
            if arriving:
                load_kv(index).wait()
            place = pl.ds(pl.multiple_of(index * chunk, chunk), chunk)
            part = jnp.dot(queries, kv[:, place], preferred_element_type=F32) * score_scale
            column = lax.broadcasted_iota(jnp.int32, (1, chunk), 1) + index * chunk
            part = jnp.where(column < length, part, -jnp.inf)
            scores[rows, place] = part
            highest = peak[rows, :]
            for k in range(0, chunk, 128):
                highest = jnp.maximum(highest, part[:, k : k + 128])
            peak[rows, :] = highest

        top = jnp.max(peak[rows, :], axis=1, keepdims=True)
        peak[rows, :] = jnp.broadcast_to(top, (rows.size, 128))
        total[rows, :] = jnp.zeros((rows.size, 128), F32)
        old[rows, :] = jnp.zeros((rows.size, lat), F32)

        @pl.loop(0, chunks)
        def _(index):
            place = pl.ds(pl.multiple_of(index * chunk, chunk), chunk)
            weights = jnp.exp(scores[rows, place] - peak[rows, :1])
            running = total[rows, :]
            for k in range(0, chunk, 128):
                running = running + weights[:, k : k + 128]
            total[rows, :] = running
            old[rows, :] += lax.dot_general(
                weights.astype(BF16), kv[:lat, place], NT, preferred_element_type=F32
            )

        sums = jnp.sum(total[rows, :], axis=1, keepdims=True)
        total[rows, :] = jnp.broadcast_to(sums, (rows.size, 128))

    def head_rows(s):
        start = s * head_count
        return pl.ds(start if isinstance(s, int) else pl.multiple_of(start, head_count), head_count)

    def send_old(s):
        rows = head_rows(s)
        whole = old[rows, :] / total[rows, :1]
        for h in range(head_count):
            o_send[s, h] = whole[h : h + 1, :]
        mine = pl.ds(z * per, per)
        o_recv[s, :, z] = o_send[s, mine]

        @pl.loop(0, nz - 1)
        def _(i):
            peer, device = z_peer(i)
            theirs = pl.ds(peer * per, per)
            push(
                o_send.at[s, theirs], o_recv.at[s, :, z], o_sent.at[s], o_sem.at[s], device
            ).start()

    wide = half_per * lat // 2
    sides = [pl.ds(0, wide), pl.ds(wide, wide)]

    def build_old(s):
        await_bytes(o_sem.at[s], o_send.at[s, pl.ds(0, per * (nz - 1))])
        await_bytes(o_sent.at[s], o_send.at[s, pl.ds(0, per * (nz - 1))])
        for h in range(half_per):
            pair = [o_recv[s, k * half_per + h, :, 0, :] for k in range(2)]
            old_heads[s, t, :, h * lat : (h + 1) * lat] = jnp.concatenate(pair, axis=0).astype(BF16)

    def share_old(s, part):
        @pl.loop(0, nt - 1)
        def _(i):
            piece = old_heads.at[s, t, :, sides[part]]
            push(piece, piece, p_sent.at[2 * s + part], p_sem.at[2 * s + part], t_peer(i)[1]).start()

    def await_old(s, count):
        for part in range(2):
            piece = old_heads.at[s, pl.ds(0, count), :, sides[part]]
            await_bytes(p_sem.at[2 * s + part], piece)
            await_bytes(p_sent.at[2 * s + part], piece)

    def start_keys(s):
        landed(0, first(a_recv, nt - 1))
        sent(0, first(a_send, nt - 1))
        raw = jnp.sum(a_recv[...], axis=0)
        inverse = lax.rsqrt(raw[:, lat + 128 : lat + 129] / width + norm_eps)
        raw = raw * inverse
        content = raw[:, :lat]
        spread = jnp.mean(content * content, axis=1, keepdims=True)
        content = content * lax.rsqrt(spread + norm_eps) * kg_ref[...]
        rope = raw[:, lat : lat + 128]
        half = (key_width - lat) // 2
        lane = lax.broadcasted_iota(jnp.int32, (1, 128), 1)
        turned = jnp.where(
            lane < half, -pltpu.roll(rope, 128 - half, 1), pltpu.roll(rope, half, 1)
        )
        now = pl.ds(s, 1)
        rope = rope * turns[0, now, :] + turned * turns[1, now, :]
        latent = jnp.concatenate([content, rope], axis=1)[:, :key_width].astype(BF16)
        lat_out[s] = latent
        fresh[pl.ds(s, 1), :] = latent.astype(F32)

        keys = fresh[...].astype(BF16)
        recent = lax.dot_general(q_ref[s], keys, NT, preferred_element_type=F32) * score_scale
        column = lax.broadcasted_iota(jnp.int32, recent.shape, 1)
        recent = jnp.where(column <= s, recent, -jnp.inf)
        own = head_rows(s)
        top_old = peak[own, :1]
        highest = jnp.maximum(top_old, jnp.max(recent, axis=1, keepdims=True))
        weight_old = total[own, :1] * jnp.exp(top_old - highest)
        weight_new = jnp.exp(recent - highest)
        denominator = weight_old + jnp.sum(weight_new, axis=1, keepdims=True)
        share_new = (weight_new / denominator).astype(BF16).astype(F32)
        column = lax.broadcasted_iota(jnp.int32, (head_count, 128), 1)
        table = jnp.where(column == 0, weight_old / denominator, 0.0)
        for j in range(steps):
            table = jnp.where(column == j + 1, share_new[:, j : j + 1], table)
        table = jnp.concatenate([table, jnp.zeros((128 - head_count, 128), F32)], axis=0).T
        b_send[0, :, :lat] = latent[:, :lat].astype(F32)
        for k in range(steps + 1):
            b_send[0, :, lat + k * 128 : lat + (k + 1) * 128] = table[k : k + 1, :]
        b_recv[z] = b_send[0]
        send(1, z_peer, nz, lambda peer: b_send.at[0], b_recv.at[z])
    def share_keys(s):
        landed(1, first(b_recv, nz - 1))
        sent(1, first(b_recv, nz - 1))
        news = b_recv[:, 0, :]
        lane = lax.broadcasted_iota(jnp.int32, (nz, 128), 1)
        coarse = jnp.zeros((nz, 128), F32)
        for k in range(steps + 1):
            moved = pltpu.roll(
                news[:, lat + k * 128 : lat + (k + 1) * 128],
                lax.rem(k * per - z * per + 128, 128),
                1,
            )
            coarse = jnp.where((lane >= k * per) & (lane < (k + 1) * per), moved, coarse)
        fine = coarse - coarse.astype(BF16).astype(F32)
        upper = jnp.concatenate([news[:, : lat // 2], coarse], axis=1)
        lower = jnp.concatenate([news[:, lat // 2 : lat], fine], axis=1)
        l_all[t] = jnp.concatenate([upper, lower], axis=0).astype(BF16)
        send(2, t_peer, nt, lambda peer: l_all.at[t], l_all.at[t])
    attend(0, 1, True)
    send_old(0)
    start_keys(0)
    build_old(0)
    first_hop = ((x_peer, sides[0]), (y_peer, sides[1]))
    for part, (peer_of, cols) in enumerate(first_hop):

        @pl.loop(0, side - 1)
        def _(i, part=part, peer_of=peer_of, cols=cols):
            piece = old_heads.at[0, t, :, cols]
            push(piece, piece, q_sem.at[part], q_sem.at[2 + part], peer_of(i)[1]).start()

    share_keys(0)
    for part, (_, cols) in enumerate(first_hop):
        await_bytes(q_sem.at[2 + part], old_heads.at[0, pl.ds(0, side - 1), :, cols])
        await_bytes(q_sem.at[part], old_heads.at[0, pl.ds(0, side - 1), :, cols])

    @pl.loop(0, side - 1)
    def _(i):
        for j in range(side):
            piece = old_heads.at[0, j * side + yy, :, sides[0]]
            push(piece, piece, p_sent.at[0], p_sem.at[0], y_peer(i)[1]).start()
        piece = old_heads.at[0, pl.ds(xx * side, side), :, sides[1]]
        push(piece, piece, p_sent.at[1], p_sem.at[1], x_peer(i)[1]).start()

    attend(1, steps, False)

    @pl.loop(1, steps)
    def _(s):
        send_old(s)

    for one in own_weights:
        one.wait()
    for one in swaps:
        one.wait()
    for source, target in ((wo, wo_rows), (wd, wd_rows)):
        size = min(256, source.shape[2] // 2)
        while source.shape[2] % size:
            size -= 128
        for k in range(2):

            @pl.loop(0, source.shape[2] // size)
            def _(i):
                place = pl.ds(pl.multiple_of(i * size, size), size)
                target[k, place, :] = source[k, :, place].T
    await_old(0, side * (side - 1))

    @pl.loop(0, steps)
    def _(s):
        landed(2, first(l_all, nt - 1))
        sent(2, first(l_all, nt - 1))

        news = l_all[...].astype(F32)
        upper = news[:, :nz, :].reshape(nt * nz, -1)
        lower = news[:, nz:, :].reshape(nt * nz, -1)
        latents[s] = jnp.concatenate([upper[:, : lat // 2], lower[:, : lat // 2]], axis=1)
        table = upper[:, lat // 2 :] + lower[:, lat // 2 :]
        for h in range(half_per):
            pair = old_heads[s, :, :, h * lat : (h + 1) * lat].astype(F32)
            for k in range(2):
                number = k * half_per + h
                joined = pair[:, k * nz : (k + 1) * nz, :].reshape(nt * nz, lat)
                joined = joined * table[:, number : number + 1]
                for j in range(steps):
                    at = (j + 1) * per + number
                    joined = joined + latents[j] * table[:, at : at + 1]
                heads[k, :, h * lat : (h + 1) * lat] = joined.astype(BF16)

        for part, (low, high) in enumerate(parts):
            cols = pl.ds(low, high - low)
            attended = sum(
                jnp.dot(heads[k], wo_rows[k, :, low:high], preferred_element_type=F32)
                for k in range(2)
            )
            for k in range(low, high, 128):
                size = min(128, high - k)
                y_rows[k // 128, :, :size] = attended[:, k - low : k - low + size]
            for i in range(nz):
                for k in range(low, high, 128):
                    size = min(128, high - k)
                    picked = y_rows[k // 128, pl.ds(i, nt, stride=nz), :]
                    y_send[i, :, k : k + size] = picked[:, :size].astype(BF16)
            y_recv[z, :, cols] = y_send[z, :, cols]
            send(
                3 + part,
                z_peer,
                nz,
                lambda peer, cols=cols: y_send.at[peer, :, cols],
                y_recv.at[z, :, cols],
            )

        @pl.when(s < steps - 1)
        def _():
            build_old(s + 1)
            share_old(s + 1, 0)

        for part, (low, high) in enumerate(parts):
            cols = pl.ds(low, high - low)
            landed(3 + part, y_recv.at[pl.ds(0, nz - 1), :, cols])
            residual = states[:, cols] + jnp.sum(y_recv[:, :, cols].astype(F32), axis=0)
            resid[:, cols] = residual
            mine = normed.at[pl.ds(pl.multiple_of(z * nt, nt), nt), cols]
            mine[...] = (residual * mg_ref[:, cols]).astype(BF16)
            send(5 + part, z_peer, nz, lambda peer, mine=mine: mine, mine)
        for part, (low, high) in enumerate(parts):
            cols = pl.ds(low, high - low)
            landed(5 + part, normed.at[pl.ds(0, nt * (nz - 1)), cols])
            sent(3 + part, y_send.at[pl.ds(0, nz - 1), :, cols])
            sent(5 + part, normed.at[pl.ds(0, nt * (nz - 1)), cols])

        rows = normed[...]
        unscaled = rows.astype(F32) * mg_inv[...]
        squares = jnp.sum(unscaled * unscaled, axis=1, keepdims=True)
        coarse = squares.astype(BF16).astype(F32)
        lane = lax.broadcasted_iota(jnp.int32, (nt * nz, 128), 1)
        pair = jnp.where(lane < 64, coarse, squares - coarse).astype(BF16)
        for i in range(nt):
            here = i // 2 * nt
            gate_send[i // side, i % side, :, :128] = pair[here : here + nt, :]
        halves = ((0, cut), (cut, ff))
        gate_cols = [pl.ds(0, 128 + cut), pl.ds(128 + cut, ff - cut)]
        up_cols = [pl.ds(0, cut), pl.ds(cut, ff - cut)]

        def three(ref, cols):
            return ref.at[pl.ds(0, side - 1), :, :, cols]

        def three_mid(ref, cols):
            return ref.at[pl.ds(0, side - 1), :, cols]

        for part, (low, high) in enumerate(halves):
            cols = gate_cols[part]
            for k in range(2):
                gate = jnp.dot(rows, wgu[k, 0, :, low:high], preferred_element_type=F32)
                gate = gate.astype(BF16)
                for i in range(nz):
                    place = 2 * i + k
                    gate_send[place // side, place % side, :, 128 + low : 128 + high] = gate[
                        i * nt : (i + 1) * nt, :
                    ]
            gate_recv[xx, :, :, cols] = gate_send[xx, :, :, cols]
            send(
                7 + part,
                x_peer,
                side,
                lambda peer, cols=cols: gate_send.at[peer, :, :, cols],
                gate_recv.at[xx, :, :, cols],
            )
            cols = up_cols[part]
            for k in range(2):
                up = jnp.dot(rows, wgu[k, 1, :, low:high], preferred_element_type=F32)
                up = up.astype(BF16)
                for i in range(nz):
                    place = 2 * i + k
                    up_send[place % side, place // side, :, low:high] = up[i * nt : (i + 1) * nt, :]
            up_recv[yy, :, :, cols] = up_send[yy, :, :, cols]
            send(
                9 + part,
                y_peer,
                side,
                lambda peer, cols=cols: up_send.at[peer, :, :, cols],
                up_recv.at[yy, :, :, cols],
            )
        for part in range(2):
            cols = gate_cols[part]
            landed(7 + part, three(gate_recv, cols))
            for i in range(side):
                gate_mid[i, :, cols] = jnp.sum(gate_recv[:, i, :, cols].astype(F32), axis=0).astype(
                    BF16
                )
            gate_last[yy, :, cols] = gate_mid[yy, :, cols]
            send(
                11 + part,
                y_peer,
                side,
                lambda peer, cols=cols: gate_mid.at[peer, :, cols],
                gate_last.at[yy, :, cols],
            )
            cols = up_cols[part]
            landed(9 + part, three(up_recv, cols))
            for i in range(side):
                up_mid[i, :, cols] = jnp.sum(up_recv[:, i, :, cols].astype(F32), axis=0).astype(
                    BF16
                )
            up_last[xx, :, cols] = up_mid[xx, :, cols]
            send(
                13 + part,
                x_peer,
                side,
                lambda peer, cols=cols: up_mid.at[peer, :, cols],
                up_last.at[xx, :, cols],
            )
        place = lax.rem(t, 2) * nz + t // 2
        inverse = None
        for part, (low, high) in enumerate(halves):
            cols = gate_cols[part]
            landed(11 + part, three_mid(gate_last, cols))
            gate = jnp.sum(gate_last[:, :, cols].astype(F32), axis=0)
            if part == 0:
                squares = jnp.sum(gate[:, :128], axis=1, keepdims=True) / 64
                inverse = lax.rsqrt(squares / width + norm_eps)
                gate = gate[:, 128:]
            gate = gate * inverse
            gate = gate * jax.nn.sigmoid(gate) * inverse
            cols = up_cols[part]
            landed(13 + part, three_mid(up_last, cols))
            up = jnp.sum(up_last[:, :, cols].astype(F32), axis=0)
            mine = hidden.at[pl.ds(pl.multiple_of(place * nt, nt), nt), cols]
            mine[...] = (gate * up).astype(BF16)
            send(15 + part, t_peer, nt, lambda peer, mine=mine: mine, mine)
        for part in range(2):
            sent(7 + part, three(gate_send, gate_cols[part]))
            sent(9 + part, three(up_send, up_cols[part]))
            sent(11 + part, three_mid(gate_mid, gate_cols[part]))
            sent(13 + part, three_mid(up_mid, up_cols[part]))

        landed(15, hidden.at[pl.ds(0, nt * (nt - 1)), up_cols[0]])
        half_rows = nz * nt
        early = sum(
            jnp.dot(
                hidden[k * half_rows : (k + 1) * half_rows, :cut],
                wd_rows[k, :cut, :],
                preferred_element_type=F32,
            )
            for k in range(2)
        )
        landed(16, hidden.at[pl.ds(0, nt * (nt - 1)), up_cols[1]])
        for part, (low, high) in enumerate(parts):
            cols = pl.ds(low, high - low)
            down = early[:, low:high] + sum(
                jnp.dot(
                    hidden[k * half_rows : (k + 1) * half_rows, cut:],
                    wd_rows[k, cut:, low:high],
                    preferred_element_type=F32,
                )
                for k in range(2)
            )
            d_send[:, cols] = down.astype(BF16)
            d_recv[z, :, cols] = d_send[pl.ds(pl.multiple_of(z * nt, nt), nt), cols]
            send(
                17 + part,
                z_peer,
                nz,
                lambda peer, cols=cols: d_send.at[
                    pl.ds(pl.multiple_of(peer * nt, nt), nt), cols
                ],
                d_recv.at[z, :, cols],
            )
        @pl.when(s < steps - 1)
        def _():
            share_old(s + 1, 1)

        for part in range(2):
            sent(15 + part, hidden.at[pl.ds(0, nt * (nt - 1)), up_cols[part]])
        for part, (low, high) in enumerate(parts):
            cols = pl.ds(low, high - low)
            landed(17 + part, d_recv.at[pl.ds(0, nz - 1), :, cols])
            sent(17 + part, d_send.at[pl.ds(0, nt * (nz - 1)), cols])
        mixed = (resid[...] + jnp.sum(d_recv[...].astype(F32), axis=0)).astype(BF16)
        out_ref[s] = mixed
        states[...] = mixed.astype(F32)

        @pl.when(s < steps - 1)
        def _():
            send_latent()
            start_keys(s + 1)
            share_keys(s + 1)
            await_old(s + 1, nt - 1)


def body(token_states, queries, kv_cache, lengths, attn_gain, kv_gain, w_latent, w_out, mlp_gain, w_gate_up, w_down):
    nt, width = token_states.shape
    nz = nt // 2
    side = int(round(nt**0.5))
    steps, _, head_count, key_width = queries.shape
    slots = kv_cache.shape[1]
    lat = kv_gain.shape[0]
    ff = w_down.shape[0]
    depth = w_out.shape[0]
    per = head_count // nz
    half = (key_width - lat) // 2
    frequency = np.zeros((1, 128), np.float32)
    frequency[0, : 2 * half] = np.tile(10000.0 ** (-np.arange(half) / half), 2)
    chunk = min(512, slots)
    rows = steps * head_count
    vmem = pl.BlockSpec(memory_space=pltpu.VMEM)
    hbm = pl.BlockSpec(memory_space=pl.ANY)
    news = lat + (steps + 1) * 128
    block = lat // 2 + 128
    mixed, latents = pl.pallas_call(
        functools.partial(layer_kernel, float(width * lax.axis_size("tp"))),
        out_shape=(
            jax.ShapeDtypeStruct((steps, nt, width), BF16),
            jax.ShapeDtypeStruct((steps, 1, key_width), BF16),
        ),
        in_specs=[hbm, hbm, pl.BlockSpec(memory_space=pltpu.SMEM)] + [hbm] * 9,
        out_specs=(vmem, vmem),
        scratch_shapes=[
            pltpu.VMEM((nt, width), BF16),
            pltpu.VMEM((steps, head_count, key_width), BF16),
            pltpu.VMEM((1, width), F32),
            pltpu.VMEM((1, lat), F32),
            pltpu.VMEM((1, width), F32),
            pltpu.VMEM((1, 128), F32),
            pltpu.VMEM((key_width, slots), BF16),
            pltpu.VMEM(w_latent.shape, BF16),
            pltpu.VMEM((2, width, depth), BF16),
            pltpu.VMEM((2,) + w_gate_up.shape, BF16),
            pltpu.VMEM((2, width, ff), BF16),
            pltpu.VMEM((2, depth, width), BF16),
            pltpu.VMEM((2, ff, width), BF16),
            pltpu.VMEM((2, 8, 128), F32),
            pltpu.VMEM((1, width), F32),
            pltpu.VMEM((rows, slots), F32),
            pltpu.VMEM((rows, 128), F32),
            pltpu.VMEM((rows, 128), F32),
            pltpu.VMEM((rows, lat), F32),
            pltpu.VMEM((nt, width), F32),
            pltpu.VMEM((nt, width), F32),
            pltpu.VMEM((16, key_width), F32),
            pltpu.VMEM((nt, lat + 256), F32),
            pltpu.VMEM((nt, 1, lat + 256), F32),
            pltpu.VMEM((nt, 1, lat + 256), F32),
            pltpu.VMEM((steps, head_count, 1, lat), F32),
            pltpu.VMEM((steps, per, nz, 1, lat), F32),
            pltpu.VMEM((steps, nt, 2 * nz, per // 2 * lat), BF16),
            pltpu.VMEM((1, 1, news), F32),
            pltpu.VMEM((nz, 1, news), F32),
            pltpu.VMEM((nt, 2 * nz, block), BF16),
            pltpu.VMEM((steps, nt * nz, lat), F32),
            pltpu.VMEM((2, nt * nz, depth), BF16),
            pltpu.VMEM((-(-width // 128), nt * nz, 128), F32),
            pltpu.VMEM((nz, nt, width), BF16),
            pltpu.VMEM((nz, nt, width), BF16),
            pltpu.VMEM((nz * nt, width), BF16),
            pltpu.VMEM((side, side, nt, ff + 128), BF16),
            pltpu.VMEM((side, side, nt, ff + 128), BF16),
            pltpu.VMEM((side, nt, ff + 128), BF16),
            pltpu.VMEM((side, nt, ff + 128), BF16),
            pltpu.VMEM((side, side, nt, ff), BF16),
            pltpu.VMEM((side, side, nt, ff), BF16),
            pltpu.VMEM((side, nt, ff), BF16),
            pltpu.VMEM((side, nt, ff), BF16),
            pltpu.VMEM((nt * nt, ff), BF16),
            pltpu.VMEM((nz * nt, width), BF16),
            pltpu.VMEM((nz, nt, width), BF16),
            pltpu.SemaphoreType.DMA((10 + slots // chunk,)),
            pltpu.SemaphoreType.DMA((3,)),
            pltpu.SemaphoreType.DMA((3,)),
            pltpu.SemaphoreType.DMA((19,)),
            pltpu.SemaphoreType.DMA((19,)),
            pltpu.SemaphoreType.DMA((steps,)),
            pltpu.SemaphoreType.DMA((steps,)),
            pltpu.SemaphoreType.DMA((2 * steps,)),
            pltpu.SemaphoreType.DMA((2 * steps,)),
            pltpu.SemaphoreType.DMA((4,)),
        ],
        compiler_params=pltpu.CompilerParams(
            collective_id=0, has_side_effects=True, vmem_limit_bytes=56 * 1024 * 1024
        ),
        name="decode_layer",
    )(
        token_states,
        queries.reshape(steps, head_count, key_width),
        lengths,
        attn_gain.reshape(1, -1),
        kv_gain.reshape(1, -1),
        mlp_gain.reshape(1, -1),
        jnp.asarray(frequency),
        kv_cache.reshape(slots, key_width).T,
        w_latent,
        w_out.T,
        w_gate_up,
        w_down.T,
    )
    return mixed, latents


def solution(mesh):
    placed = (
        P("dp", "tp"),
        P(None, ("dp", "tp"), None, None),
        P(("dp", "tp"), None, None),
        P(("dp", "tp")),
        P("tp"),
        P(),
        P("tp", None),
        P("dp", "tp"),
        P("tp"),
        P(None, "tp", "dp"),
        P("dp", "tp"),
    )
    return jax.shard_map(
        body,
        mesh=mesh,
        in_specs=placed,
        out_specs=(P(None, "dp", "tp"), P(None, ("dp", "tp"), None)),
        check_vma=False,
    )
```

```python
import functools

import jax
import jax.numpy as jnp
import numpy as np
from jax import lax
from jax.experimental import pallas as pl
from jax.experimental.pallas import tpu as pltpu
from jax.sharding import PartitionSpec as P

D = 7168
norm_eps = 1e-06
score_scale = 192.0 ** (-0.5)
MESH = pl.DeviceIdType.MESH
F32 = jnp.float32
BF16 = jnp.bfloat16
NT = (((1,), (1,)), ((), ()))


def layer_kernel(
    width,
    x_hbm,
    q_hbm,
    len_ref,
    ag_hbm,
    kg_hbm,
    mg_hbm,
    freq_hbm,
    kv_hbm,
    wl_hbm,
    wo_hbm,
    wgu_hbm,
    wd_hbm,
    out_ref,
    lat_out,
    x_ref,
    q_ref,
    ag_ref,
    kg_ref,
    mg_ref,
    freq_ref,
    kv,
    wl,
    wo,
    wgu,
    wd,
    wo_rows,
    wd_rows,
    turns,
    mg_inv,
    scores,
    peak,
    total,
    peak_rows,
    total_rows,
    old,
    states,
    resid,
    fresh,
    a_rows,
    a_send,
    a_recv,
    o_send,
    o_recv,
    old_heads,
    b_send,
    b_recv,
    l_all,
    latents,
    heads,
    y_rows,
    y_send,
    y_recv,
    normed,
    gate_send,
    gate_recv,
    gate_mid,
    gate_last,
    up_send,
    up_recv,
    up_mid,
    up_last,
    hidden,
    d_send,
    d_recv,
    load_sem,
    swap_send,
    swap_recv,
    send_sem,
    recv_sem,
    o_sem,
    o_sent,
    p_sem,
    p_sent,
    q_sem,
):
    nt = x_ref.shape[0]
    nz = nt // 2
    side = gate_recv.shape[0]
    steps, head_count, key_width = q_ref.shape
    lat = kg_ref.shape[1]
    ff = wd.shape[2]
    share = wd.shape[1]
    slots = kv.shape[1]
    per = head_count // nz
    half_per = per // 2
    cut = ff // 256 * 128
    middle = (share + 255) // 256 * 128
    parts = ((0, middle), (middle, share)) if middle < share else ((0, share),)
    chunks = load_sem.shape[0] - 10
    chunk = slots // chunks
    g = lax.axis_index("dp")
    z = g // 2
    c = lax.rem(g, 2)
    t = lax.axis_index("tp")
    xx = t // side
    yy = lax.rem(t, side)
    sibling = (z * 2 + 1 - c, t)

    def away(k, count):
        odd = lax.rem(k, 2)
        return count // 2 + k // 2 * (1 - odd) - (k + 1) // 2 * odd

    def z_peer(k):
        peer = lax.rem(z + away(k, nz), nz)
        return peer, (peer * 2 + c, t)

    def t_peer(k):
        px = lax.rem(xx + away(k // side, side), side)
        py = lax.rem(yy + away(lax.rem(k, side), side), side)
        peer = px * side + py
        return peer, (g, peer)

    def x_peer(k):
        peer = lax.rem(xx + away(k, side), side)
        return peer, (g, peer * side + yy)

    def y_peer(k):
        peer = lax.rem(yy + away(k, side), side)
        return peer, (g, xx * side + peer)

    def load(source, target, index):
        return pltpu.make_async_copy(source, target, load_sem.at[index])

    loads = [
        load(x_hbm, x_ref, 0),
        load(ag_hbm, ag_ref, 1),
        load(wl_hbm, wl, 2),
        load(q_hbm, q_ref, 3),
        load(kg_hbm, kg_ref, 4),
        load(freq_hbm, freq_ref, 5),
        load(mg_hbm, mg_ref, 6),
    ]
    for one in loads:
        one.start()

    def load_kv(index):
        place = pl.ds(pl.multiple_of(index * chunk, chunk), chunk)
        return load(kv_hbm.at[:, place], kv.at[:, place], 10 + index)

    @pl.loop(0, chunks)
    def _(index):
        load_kv(index).start()

    own_weights = [
        load(wo_hbm, wo.at[c], 7),
        load(wgu_hbm, wgu.at[c], 8),
        load(wd_hbm, wd.at[c], 9),
    ]
    for one in own_weights:
        one.start()

    barrier = pltpu.get_barrier_semaphore()

    @pl.loop(0, nz - 1)
    def _(i):
        pl.semaphore_signal(barrier, inc=1, device_id=z_peer(i)[1], device_id_type=MESH)

    @pl.loop(0, nt - 1)
    def _(i):
        pl.semaphore_signal(barrier, inc=1, device_id=t_peer(i)[1], device_id_type=MESH)

    pl.semaphore_signal(barrier, inc=1, device_id=sibling, device_id_type=MESH)
    pl.semaphore_wait(barrier, nz + nt - 1)

    def push(source, target, sent, landed, device):
        return pltpu.make_async_remote_copy(
            src_ref=source,
            dst_ref=target,
            send_sem=sent,
            recv_sem=landed,
            device_id=device,
            device_id_type=MESH,
        )

    swaps = [
        push(source, target.at[c], swap_send.at[k], swap_recv.at[k], sibling)
        for k, (source, target) in enumerate(((wo_hbm, wo), (wgu_hbm, wgu), (wd_hbm, wd)))
    ]

    def send(phase, peer_of, count, source, target):
        @pl.loop(0, count - 1)
        def _(i):
            peer, device = peer_of(i)
            push(source(peer), target, send_sem.at[phase], recv_sem.at[phase], device).start()

    def await_bytes(sem, ref):
        pltpu.make_async_copy(ref, ref, sem).wait()

    def block(ref, index):
        return ref.at[pl.ds(pl.multiple_of(index * nt, nt), nt)]

    def first(ref, count):
        return ref.at[pl.ds(0, count)]

    def landed(phase, ref):
        await_bytes(recv_sem.at[phase], ref)

    def sent(phase, ref):
        await_bytes(send_sem.at[phase], ref)

    def send_latent():
        xs = states[...]
        scaled = (xs * ag_ref[...]).astype(BF16)
        a_rows[:, :key_width] = jnp.dot(scaled, wl[...], preferred_element_type=F32)
        squares = jnp.sum(xs * xs, axis=1, keepdims=True)
        a_rows[:, lat + 128 :] = jnp.broadcast_to(squares, (nt, 128))
        for i in range(nt):
            a_send[i] = a_rows[i : i + 1, :]
        a_recv[t] = a_send[t]
        send(0, t_peer, nt, lambda peer: a_send.at[peer], a_recv.at[t])

    a_rows[...] = jnp.zeros_like(a_rows)
    fresh[...] = jnp.zeros_like(fresh)
    latents[...] = jnp.zeros_like(latents)
    b_send[...] = jnp.zeros_like(b_send)
    for one in loads[:3]:
        one.wait()
    states[...] = x_ref[...].astype(F32)
    send_latent()
    for one in swaps:
        one.start()

    length = len_ref[0]
    for one in loads[3:]:
        one.wait()
    row = lax.broadcasted_iota(jnp.int32, turns.shape[1:], 0)
    angles = (row + length).astype(F32) * freq_ref[...]
    turns[0] = jnp.cos(angles)
    turns[1] = jnp.sin(angles)
    mg_inv[...] = 1.0 / mg_ref[...]

    def attend(low, high, arriving):
        rows = pl.ds(low * head_count, (high - low) * head_count)
        queries = q_ref[low:high].reshape((high - low) * head_count, key_width)
        peak[rows, :] = jnp.full((rows.size, 128), -jnp.inf, F32)

        @pl.loop(0, chunks)
        def _(index):
            if arriving:
                load_kv(index).wait()
            place = pl.ds(pl.multiple_of(index * chunk, chunk), chunk)
            part = jnp.dot(queries, kv[:, place], preferred_element_type=F32) * score_scale
            column = lax.broadcasted_iota(jnp.int32, (1, chunk), 1) + index * chunk
            part = jnp.where(column < length, part, -jnp.inf)
            scores[rows, place] = part
            highest = peak[rows, :]
            for k in range(0, chunk, 128):
                highest = jnp.maximum(highest, part[:, k : k + 128])
            peak[rows, :] = highest

        top = jnp.max(peak[rows, :], axis=1, keepdims=True)
        peak[rows, :] = jnp.broadcast_to(top, (rows.size, 128))
        total[rows, :] = jnp.zeros((rows.size, 128), F32)
        old[rows, :] = jnp.zeros((rows.size, lat), F32)

        @pl.loop(0, chunks)
        def _(index):
            place = pl.ds(pl.multiple_of(index * chunk, chunk), chunk)
            weights = jnp.exp(scores[rows, place] - peak[rows, :1])
            running = total[rows, :]
            for k in range(0, chunk, 128):
                running = running + weights[:, k : k + 128]
            total[rows, :] = running
            old[rows, :] += lax.dot_general(
                weights.astype(BF16), kv[:lat, place], NT, preferred_element_type=F32
            )

        sums = jnp.sum(total[rows, :], axis=1, keepdims=True)
        total[rows, :] = jnp.broadcast_to(sums, (rows.size, 128))
        rest = jnp.zeros((128 - head_count, 128), F32)
        for s in range(low, high):
            here = pl.ds(s * head_count, head_count)
            peak_rows[s] = jnp.concatenate([peak[here, :], rest], axis=0).T[:1, :]
            total_rows[s] = jnp.concatenate([total[here, :], rest], axis=0).T[:1, :]

    def head_rows(s):
        start = s * head_count
        return pl.ds(start if isinstance(s, int) else pl.multiple_of(start, head_count), head_count)

    def send_old(s):
        rows = head_rows(s)
        whole = old[rows, :] / total[rows, :1]
        for h in range(head_count):
            o_send[s, h] = whole[h : h + 1, :]
        mine = pl.ds(z * per, per)
        o_recv[s, :, z] = o_send[s, mine]

        @pl.loop(0, nz - 1)
        def _(i):
            peer, device = z_peer(i)
            theirs = pl.ds(peer * per, per)
            push(
                o_send.at[s, theirs], o_recv.at[s, :, z], o_sent.at[s], o_sem.at[s], device
            ).start()

    wide = half_per * lat // 2
    sides = [pl.ds(0, wide), pl.ds(wide, wide)]

    def build_old(s):
        await_bytes(o_sem.at[s], o_send.at[s, pl.ds(0, per * (nz - 1))])
        await_bytes(o_sent.at[s], o_send.at[s, pl.ds(0, per * (nz - 1))])
        for h in range(half_per):
            pair = [o_recv[s, k * half_per + h, :, 0, :] for k in range(2)]
            old_heads[s, t, :, h * lat : (h + 1) * lat] = jnp.concatenate(pair, axis=0).astype(BF16)

    def share_old(s, part):
        @pl.loop(0, nt - 1)
        def _(i):
            piece = old_heads.at[s, t, :, sides[part]]
            push(piece, piece, p_sent.at[2 * s + part], p_sem.at[2 * s + part], t_peer(i)[1]).start()

    def await_old(s, count):
        for part in range(2):
            piece = old_heads.at[s, pl.ds(0, count), :, sides[part]]
            await_bytes(p_sem.at[2 * s + part], piece)
            await_bytes(p_sent.at[2 * s + part], piece)

    def start_keys(s):
        landed(0, first(a_recv, nt - 1))
        sent(0, first(a_send, nt - 1))
        raw = jnp.sum(a_recv[...], axis=0)
        inverse = lax.rsqrt(raw[:, lat + 128 : lat + 129] / width + norm_eps)
        raw = raw * inverse
        content = raw[:, :lat]
        spread = jnp.mean(content * content, axis=1, keepdims=True)
        content = content * lax.rsqrt(spread + norm_eps) * kg_ref[...]
        rope = raw[:, lat : lat + 128]
        half = (key_width - lat) // 2
        lane = lax.broadcasted_iota(jnp.int32, (1, 128), 1)
        turned = jnp.where(
            lane < half, -pltpu.roll(rope, 128 - half, 1), pltpu.roll(rope, half, 1)
        )
        now = pl.ds(s, 1)
        rope = rope * turns[0, now, :] + turned * turns[1, now, :]
        latent = jnp.concatenate([content, rope], axis=1)[:, :key_width].astype(BF16)
        fresh[pl.ds(s, 1), :] = latent.astype(F32)

        keys = fresh[...].astype(BF16)
        recent = lax.dot_general(keys, q_ref[s], NT, preferred_element_type=F32) * score_scale
        place = lax.broadcasted_iota(jnp.int32, recent.shape, 0)
        recent = jnp.where(place <= s, recent, -jnp.inf)
        top_old = peak_rows[s, :, :head_count]
        highest = jnp.maximum(top_old, jnp.max(recent, axis=0, keepdims=True))
        weight_old = total_rows[s, :, :head_count] * jnp.exp(top_old - highest)
        weight_new = jnp.exp(recent - highest)
        denominator = weight_old + jnp.sum(weight_new, axis=0, keepdims=True)
        share_new = (weight_new / denominator).astype(BF16).astype(F32)
        b_send[0, :, :lat] = latent[:, :lat].astype(F32)
        b_send[0, :, lat : lat + head_count] = weight_old / denominator
        for k in range(steps):
            start = lat + (k + 1) * 128
            b_send[0, :, start : start + head_count] = share_new[k : k + 1, :]
        b_recv[z] = b_send[0]
        send(1, z_peer, nz, lambda peer: b_send.at[0], b_recv.at[z])
    def share_keys(s):
        landed(1, first(b_recv, nz - 1))
        sent(1, first(b_recv, nz - 1))
        news = b_recv[:, 0, :]
        lane = lax.broadcasted_iota(jnp.int32, (nz, 128), 1)
        coarse = jnp.zeros((nz, 128), F32)
        for k in range(steps + 1):
            moved = pltpu.roll(
                news[:, lat + k * 128 : lat + (k + 1) * 128],
                lax.rem(k * per - z * per + 128, 128),
                1,
            )
            coarse = jnp.where((lane >= k * per) & (lane < (k + 1) * per), moved, coarse)
        fine = coarse - coarse.astype(BF16).astype(F32)
        upper = jnp.concatenate([news[:, : lat // 2], coarse], axis=1)
        lower = jnp.concatenate([news[:, lat // 2 : lat], fine], axis=1)
        l_all[t] = jnp.concatenate([upper, lower], axis=0).astype(BF16)
        send(2, t_peer, nt, lambda peer: l_all.at[t], l_all.at[t])
    attend(0, 1, True)
    send_old(0)
    start_keys(0)
    build_old(0)
    first_hop = ((x_peer, sides[0]), (y_peer, sides[1]))
    for part, (peer_of, cols) in enumerate(first_hop):

        @pl.loop(0, side - 1)
        def _(i, part=part, peer_of=peer_of, cols=cols):
            piece = old_heads.at[0, t, :, cols]
            push(piece, piece, q_sem.at[part], q_sem.at[2 + part], peer_of(i)[1]).start()

    share_keys(0)
    for part, (_, cols) in enumerate(first_hop):
        await_bytes(q_sem.at[2 + part], old_heads.at[0, pl.ds(0, side - 1), :, cols])
        await_bytes(q_sem.at[part], old_heads.at[0, pl.ds(0, side - 1), :, cols])

    @pl.loop(0, side - 1)
    def _(i):
        for j in range(side):
            piece = old_heads.at[0, j * side + yy, :, sides[0]]
            push(piece, piece, p_sent.at[0], p_sem.at[0], y_peer(i)[1]).start()
        piece = old_heads.at[0, pl.ds(xx * side, side), :, sides[1]]
        push(piece, piece, p_sent.at[1], p_sem.at[1], x_peer(i)[1]).start()

    attend(1, steps, False)

    @pl.loop(1, steps)
    def _(s):
        send_old(s)

    for one in own_weights:
        one.wait()
    for one in swaps:
        one.wait()
    for source, target in ((wo, wo_rows), (wd, wd_rows)):
        size = min(256, source.shape[2] // 2)
        while source.shape[2] % size:
            size -= 128
        for k in range(2):

            @pl.loop(0, source.shape[2] // size)
            def _(i):
                place = pl.ds(pl.multiple_of(i * size, size), size)
                target[k, place, :] = source[k, :, place].T
    await_old(0, side * (side - 1))

    @pl.loop(0, steps)
    def _(s):
        landed(2, first(l_all, nt - 1))
        sent(2, first(l_all, nt - 1))

        news = l_all[...].astype(F32)
        upper = news[:, :nz, :].reshape(nt * nz, -1)
        lower = news[:, nz:, :].reshape(nt * nz, -1)
        latents[s] = jnp.concatenate([upper[:, : lat // 2], lower[:, : lat // 2]], axis=1)
        table = upper[:, lat // 2 :] + lower[:, lat // 2 :]
        for h in range(half_per):
            pair = old_heads[s, :, :, h * lat : (h + 1) * lat].astype(F32)
            for k in range(2):
                number = k * half_per + h
                joined = pair[:, k * nz : (k + 1) * nz, :].reshape(nt * nz, lat)
                joined = joined * table[:, number : number + 1]
                for j in range(steps):
                    at = (j + 1) * per + number
                    joined = joined + latents[j] * table[:, at : at + 1]
                heads[k, :, h * lat : (h + 1) * lat] = joined.astype(BF16)

        for part, (low, high) in enumerate(parts):
            cols = pl.ds(low, high - low)
            attended = sum(
                jnp.dot(heads[k], wo_rows[k, :, low:high], preferred_element_type=F32)
                for k in range(2)
            )
            for k in range(low, high, 128):
                size = min(128, high - k)
                y_rows[k // 128, :, :size] = attended[:, k - low : k - low + size]
            for i in range(nz):
                for k in range(low, high, 128):
                    size = min(128, high - k)
                    picked = y_rows[k // 128, pl.ds(i, nt, stride=nz), :]
                    y_send[i, :, k : k + size] = picked[:, :size].astype(BF16)
            y_recv[z, :, cols] = y_send[z, :, cols]
            send(
                3 + part,
                z_peer,
                nz,
                lambda peer, cols=cols: y_send.at[peer, :, cols],
                y_recv.at[z, :, cols],
            )

        @pl.when(s < steps - 1)
        def _():
            build_old(s + 1)
            share_old(s + 1, 0)

        for part, (low, high) in enumerate(parts):
            cols = pl.ds(low, high - low)
            landed(3 + part, y_recv.at[pl.ds(0, nz - 1), :, cols])
            residual = states[:, cols] + jnp.sum(y_recv[:, :, cols].astype(F32), axis=0)
            resid[:, cols] = residual
            mine = normed.at[pl.ds(pl.multiple_of(z * nt, nt), nt), cols]
            mine[...] = (residual * mg_ref[:, cols]).astype(BF16)
            send(5 + part, z_peer, nz, lambda peer, mine=mine: mine, mine)
        for part, (low, high) in enumerate(parts):
            cols = pl.ds(low, high - low)
            landed(5 + part, normed.at[pl.ds(0, nt * (nz - 1)), cols])
            sent(3 + part, y_send.at[pl.ds(0, nz - 1), :, cols])
            sent(5 + part, normed.at[pl.ds(0, nt * (nz - 1)), cols])

        rows = normed[...]
        unscaled = rows.astype(F32) * mg_inv[...]
        squares = jnp.sum(unscaled * unscaled, axis=1, keepdims=True)
        coarse = squares.astype(BF16).astype(F32)
        lane = lax.broadcasted_iota(jnp.int32, (nt * nz, 128), 1)
        pair = jnp.where(lane < 64, coarse, squares - coarse).astype(BF16)
        for i in range(nt):
            here = i // 2 * nt
            gate_send[i // side, i % side, :, :128] = pair[here : here + nt, :]
        halves = ((0, cut), (cut, ff))
        gate_cols = [pl.ds(0, 128 + cut), pl.ds(128 + cut, ff - cut)]
        up_cols = [pl.ds(0, cut), pl.ds(cut, ff - cut)]

        def three(ref, cols):
            return ref.at[pl.ds(0, side - 1), :, :, cols]

        def three_mid(ref, cols):
            return ref.at[pl.ds(0, side - 1), :, cols]

        for part, (low, high) in enumerate(halves):
            cols = gate_cols[part]
            for k in range(2):
                gate = jnp.dot(rows, wgu[k, 0, :, low:high], preferred_element_type=F32)
                gate = gate.astype(BF16)
                for i in range(nz):
                    place = 2 * i + k
                    gate_send[place // side, place % side, :, 128 + low : 128 + high] = gate[
                        i * nt : (i + 1) * nt, :
                    ]
            gate_recv[xx, :, :, cols] = gate_send[xx, :, :, cols]
            send(
                7 + part,
                x_peer,
                side,
                lambda peer, cols=cols: gate_send.at[peer, :, :, cols],
                gate_recv.at[xx, :, :, cols],
            )
            cols = up_cols[part]
            for k in range(2):
                up = jnp.dot(rows, wgu[k, 1, :, low:high], preferred_element_type=F32)
                up = up.astype(BF16)
                for i in range(nz):
                    place = 2 * i + k
                    up_send[place % side, place // side, :, low:high] = up[i * nt : (i + 1) * nt, :]
            up_recv[yy, :, :, cols] = up_send[yy, :, :, cols]
            send(
                9 + part,
                y_peer,
                side,
                lambda peer, cols=cols: up_send.at[peer, :, :, cols],
                up_recv.at[yy, :, :, cols],
            )
        for part in range(2):
            cols = gate_cols[part]
            landed(7 + part, three(gate_recv, cols))
            for i in range(side):
                gate_mid[i, :, cols] = jnp.sum(gate_recv[:, i, :, cols].astype(F32), axis=0).astype(
                    BF16
                )
            gate_last[yy, :, cols] = gate_mid[yy, :, cols]
            send(
                11 + part,
                y_peer,
                side,
                lambda peer, cols=cols: gate_mid.at[peer, :, cols],
                gate_last.at[yy, :, cols],
            )
            cols = up_cols[part]
            landed(9 + part, three(up_recv, cols))
            for i in range(side):
                up_mid[i, :, cols] = jnp.sum(up_recv[:, i, :, cols].astype(F32), axis=0).astype(
                    BF16
                )
            up_last[xx, :, cols] = up_mid[xx, :, cols]
            send(
                13 + part,
                x_peer,
                side,
                lambda peer, cols=cols: up_mid.at[peer, :, cols],
                up_last.at[xx, :, cols],
            )
        place = lax.rem(t, 2) * nz + t // 2
        inverse = None
        for part, (low, high) in enumerate(halves):
            cols = gate_cols[part]
            landed(11 + part, three_mid(gate_last, cols))
            gate = jnp.sum(gate_last[:, :, cols].astype(F32), axis=0)
            if part == 0:
                squares = jnp.sum(gate[:, :128], axis=1, keepdims=True) / 64
                inverse = lax.rsqrt(squares / width + norm_eps)
                gate = gate[:, 128:]
            gate = gate * inverse
            gate = gate * jax.nn.sigmoid(gate) * inverse
            cols = up_cols[part]
            landed(13 + part, three_mid(up_last, cols))
            up = jnp.sum(up_last[:, :, cols].astype(F32), axis=0)
            mine = hidden.at[pl.ds(pl.multiple_of(place * nt, nt), nt), cols]
            mine[...] = (gate * up).astype(BF16)
            send(15 + part, t_peer, nt, lambda peer, mine=mine: mine, mine)
        for part in range(2):
            sent(7 + part, three(gate_send, gate_cols[part]))
            sent(9 + part, three(up_send, up_cols[part]))
            sent(11 + part, three_mid(gate_mid, gate_cols[part]))
            sent(13 + part, three_mid(up_mid, up_cols[part]))

        landed(15, hidden.at[pl.ds(0, nt * (nt - 1)), up_cols[0]])
        half_rows = nz * nt
        early = sum(
            jnp.dot(
                hidden[k * half_rows : (k + 1) * half_rows, :cut],
                wd_rows[k, :cut, :],
                preferred_element_type=F32,
            )
            for k in range(2)
        )
        landed(16, hidden.at[pl.ds(0, nt * (nt - 1)), up_cols[1]])
        for part, (low, high) in enumerate(parts):
            cols = pl.ds(low, high - low)
            down = early[:, low:high] + sum(
                jnp.dot(
                    hidden[k * half_rows : (k + 1) * half_rows, cut:],
                    wd_rows[k, cut:, low:high],
                    preferred_element_type=F32,
                )
                for k in range(2)
            )
            d_send[:, cols] = down.astype(BF16)
            d_recv[z, :, cols] = d_send[pl.ds(pl.multiple_of(z * nt, nt), nt), cols]
            send(
                17 + part,
                z_peer,
                nz,
                lambda peer, cols=cols: d_send.at[
                    pl.ds(pl.multiple_of(peer * nt, nt), nt), cols
                ],
                d_recv.at[z, :, cols],
            )
        @pl.when(s < steps - 1)
        def _():
            share_old(s + 1, 1)

        for part in range(2):
            sent(15 + part, hidden.at[pl.ds(0, nt * (nt - 1)), up_cols[part]])
        for part, (low, high) in enumerate(parts):
            cols = pl.ds(low, high - low)
            landed(17 + part, d_recv.at[pl.ds(0, nz - 1), :, cols])
            sent(17 + part, d_send.at[pl.ds(0, nt * (nz - 1)), cols])
        mixed = (resid[...] + jnp.sum(d_recv[...].astype(F32), axis=0)).astype(BF16)
        out_ref[s] = mixed
        states[...] = mixed.astype(F32)

        @pl.when(s < steps - 1)
        def _():
            send_latent()
            start_keys(s + 1)
            share_keys(s + 1)
            await_old(s + 1, nt - 1)

    lat_out[...] = fresh[:steps, :].astype(BF16)


def hand_out(mixed_ref, lat_ref, mixed_hbm, lat_hbm, sem):
    one = pltpu.make_async_copy(mixed_ref, mixed_hbm, sem.at[0])
    two = pltpu.make_async_copy(lat_ref, lat_hbm, sem.at[1])
    one.start()
    two.start()
    one.wait()
    two.wait()


def body(token_states, queries, kv_cache, lengths, attn_gain, kv_gain, w_latent, w_out, mlp_gain, w_gate_up, w_down):
    nt, width = token_states.shape
    nz = nt // 2
    side = int(round(nt**0.5))
    steps, _, head_count, key_width = queries.shape
    slots = kv_cache.shape[1]
    lat = kv_gain.shape[0]
    ff = w_down.shape[0]
    depth = w_out.shape[0]
    per = head_count // nz
    half = (key_width - lat) // 2
    frequency = np.zeros((1, 128), np.float32)
    frequency[0, : 2 * half] = np.tile(10000.0 ** (-np.arange(half) / half), 2)
    chunk = min(1024, slots)
    rows = steps * head_count
    vmem = pl.BlockSpec(memory_space=pltpu.VMEM)
    hbm = pl.BlockSpec(memory_space=pl.ANY)
    news = lat + (steps + 1) * 128
    block = lat // 2 + 128
    mixed, latents = pl.pallas_call(
        functools.partial(layer_kernel, float(width * lax.axis_size("tp"))),
        out_shape=(
            jax.ShapeDtypeStruct((steps, nt, width), BF16),
            jax.ShapeDtypeStruct((steps, key_width), BF16),
        ),
        in_specs=[hbm, hbm, pl.BlockSpec(memory_space=pltpu.SMEM)] + [hbm] * 9,
        out_specs=(vmem, vmem),
        scratch_shapes=[
            pltpu.VMEM((nt, width), BF16),
            pltpu.VMEM((steps, head_count, key_width), BF16),
            pltpu.VMEM((1, width), F32),
            pltpu.VMEM((1, lat), F32),
            pltpu.VMEM((1, width), F32),
            pltpu.VMEM((1, 128), F32),
            pltpu.VMEM((key_width, slots), BF16),
            pltpu.VMEM(w_latent.shape, BF16),
            pltpu.VMEM((2, width, depth), BF16),
            pltpu.VMEM((2,) + w_gate_up.shape, BF16),
            pltpu.VMEM((2, width, ff), BF16),
            pltpu.VMEM((2, depth, width), BF16),
            pltpu.VMEM((2, ff, width), BF16),
            pltpu.VMEM((2, 8, 128), F32),
            pltpu.VMEM((1, width), F32),
            pltpu.VMEM((rows, slots), F32),
            pltpu.VMEM((rows, 128), F32),
            pltpu.VMEM((rows, 128), F32),
            pltpu.VMEM((steps, 1, 128), F32),
            pltpu.VMEM((steps, 1, 128), F32),
            pltpu.VMEM((rows, lat), F32),
            pltpu.VMEM((nt, width), F32),
            pltpu.VMEM((nt, width), F32),
            pltpu.VMEM((16, key_width), F32),
            pltpu.VMEM((nt, lat + 256), F32),
            pltpu.VMEM((nt, 1, lat + 256), F32),
            pltpu.VMEM((nt, 1, lat + 256), F32),
            pltpu.VMEM((steps, head_count, 1, lat), F32),
            pltpu.VMEM((steps, per, nz, 1, lat), F32),
            pltpu.VMEM((steps, nt, 2 * nz, per // 2 * lat), BF16),
            pltpu.VMEM((1, 1, news), F32),
            pltpu.VMEM((nz, 1, news), F32),
            pltpu.VMEM((nt, 2 * nz, block), BF16),
            pltpu.VMEM((steps, nt * nz, lat), F32),
            pltpu.VMEM((2, nt * nz, depth), BF16),
            pltpu.VMEM((-(-width // 128), nt * nz, 128), F32),
            pltpu.VMEM((nz, nt, width), BF16),
            pltpu.VMEM((nz, nt, width), BF16),
            pltpu.VMEM((nz * nt, width), BF16),
            pltpu.VMEM((side, side, nt, ff + 128), BF16),
            pltpu.VMEM((side, side, nt, ff + 128), BF16),
            pltpu.VMEM((side, nt, ff + 128), BF16),
            pltpu.VMEM((side, nt, ff + 128), BF16),
            pltpu.VMEM((side, side, nt, ff), BF16),
            pltpu.VMEM((side, side, nt, ff), BF16),
            pltpu.VMEM((side, nt, ff), BF16),
            pltpu.VMEM((side, nt, ff), BF16),
            pltpu.VMEM((nt * nt, ff), BF16),
            pltpu.VMEM((nz * nt, width), BF16),
            pltpu.VMEM((nz, nt, width), BF16),
            pltpu.SemaphoreType.DMA((10 + slots // chunk,)),
            pltpu.SemaphoreType.DMA((3,)),
            pltpu.SemaphoreType.DMA((3,)),
            pltpu.SemaphoreType.DMA((19,)),
            pltpu.SemaphoreType.DMA((19,)),
            pltpu.SemaphoreType.DMA((steps,)),
            pltpu.SemaphoreType.DMA((steps,)),
            pltpu.SemaphoreType.DMA((2 * steps,)),
            pltpu.SemaphoreType.DMA((2 * steps,)),
            pltpu.SemaphoreType.DMA((4,)),
        ],
        compiler_params=pltpu.CompilerParams(
            collective_id=0, has_side_effects=True, vmem_limit_bytes=56 * 1024 * 1024
        ),
        name="decode_layer",
    )(
        token_states,
        queries.reshape(steps, head_count, key_width),
        lengths,
        attn_gain.reshape(1, -1),
        kv_gain.reshape(1, -1),
        mlp_gain.reshape(1, -1),
        jnp.asarray(frequency),
        kv_cache.reshape(slots, key_width).T,
        w_latent,
        w_out.T,
        w_gate_up,
        w_down.T,
    )
    return mixed, latents.reshape(steps, 1, key_width)


def solution(mesh):
    placed = (
        P("dp", "tp"),
        P(None, ("dp", "tp"), None, None),
        P(("dp", "tp"), None, None),
        P(("dp", "tp")),
        P("tp"),
        P(),
        P("tp", None),
        P("dp", "tp"),
        P("tp"),
        P(None, "tp", "dp"),
        P("dp", "tp"),
    )
    return jax.shard_map(
        body,
        mesh=mesh,
        in_specs=placed,
        out_specs=(P(None, "dp", "tp"), P(None, ("dp", "tp"), None)),
        check_vma=False,
    )
```

```python
import functools

import jax
import jax.numpy as jnp
import numpy as np
from jax import lax
from jax.experimental import pallas as pl
from jax.experimental.pallas import tpu as pltpu
from jax.sharding import PartitionSpec as P

D = 7168
norm_eps = 1e-06
score_scale = 192.0 ** (-0.5)
MESH = pl.DeviceIdType.MESH
F32 = jnp.float32
BF16 = jnp.bfloat16
NT = (((1,), (1,)), ((), ()))


def layer_kernel(
    width,
    x_hbm,
    q_hbm,
    len_ref,
    ag_hbm,
    kg_hbm,
    mg_hbm,
    freq_hbm,
    kv_hbm,
    wl_hbm,
    wo_hbm,
    wgu_hbm,
    wd_hbm,
    out_ref,
    lat_out,
    x_ref,
    q_ref,
    ag_ref,
    kg_ref,
    mg_ref,
    freq_ref,
    kv,
    wl,
    wo,
    wgu,
    wd,
    wo_rows,
    wd_rows,
    turns,
    mg_inv,
    scores,
    peak,
    total,
    peak_rows,
    total_rows,
    old,
    states,
    resid,
    fresh,
    a_rows,
    a_send,
    a_recv,
    o_send,
    o_recv,
    old_heads,
    b_send,
    b_recv,
    l_all,
    latents,
    heads,
    y_rows,
    y_send,
    y_recv,
    normed,
    gate_send,
    gate_recv,
    gate_mid,
    gate_last,
    up_send,
    up_recv,
    up_mid,
    up_last,
    hidden,
    d_send,
    d_recv,
    load_sem,
    swap_send,
    swap_recv,
    send_sem,
    recv_sem,
    o_sem,
    o_sent,
    p_sem,
    p_sent,
    q_sem,
):
    nt = x_ref.shape[0]
    nz = nt // 2
    side = gate_recv.shape[0]
    steps, head_count, key_width = q_ref.shape
    lat = kg_ref.shape[1]
    ff = wd.shape[2]
    share = wd.shape[1]
    slots = kv.shape[1]
    per = head_count // nz
    half_per = per // 2
    cut = ff // 256 * 128
    middle = (share + 255) // 256 * 128
    parts = ((0, middle), (middle, share)) if middle < share else ((0, share),)
    chunks = load_sem.shape[0] - 10
    chunk = slots // chunks
    g = lax.axis_index("dp")
    z = g // 2
    c = lax.rem(g, 2)
    t = lax.axis_index("tp")
    xx = t // side
    yy = lax.rem(t, side)
    sibling = (z * 2 + 1 - c, t)

    def away(k, count):
        odd = lax.rem(k, 2)
        return count // 2 + k // 2 * (1 - odd) - (k + 1) // 2 * odd

    def z_peer(k):
        peer = lax.rem(z + away(k, nz), nz)
        return peer, (peer * 2 + c, t)

    def t_peer(k):
        px = lax.rem(xx + away(k // side, side), side)
        py = lax.rem(yy + away(lax.rem(k, side), side), side)
        peer = px * side + py
        return peer, (g, peer)

    def x_peer(k):
        peer = lax.rem(xx + away(k, side), side)
        return peer, (g, peer * side + yy)

    def y_peer(k):
        peer = lax.rem(yy + away(k, side), side)
        return peer, (g, xx * side + peer)

    def load(source, target, index):
        return pltpu.make_async_copy(source, target, load_sem.at[index])

    loads = [
        load(x_hbm, x_ref, 0),
        load(ag_hbm, ag_ref, 1),
        load(wl_hbm, wl, 2),
        load(q_hbm, q_ref, 3),
        load(kg_hbm, kg_ref, 4),
        load(freq_hbm, freq_ref, 5),
        load(mg_hbm, mg_ref, 6),
    ]
    for one in loads:
        one.start()

    def load_kv(index):
        place = pl.ds(pl.multiple_of(index * chunk, chunk), chunk)
        return load(kv_hbm.at[:, place], kv.at[:, place], 10 + index)

    @pl.loop(0, chunks)
    def _(index):
        load_kv(index).start()

    own_weights = [
        load(wo_hbm, wo.at[c], 7),
        load(wgu_hbm, wgu.at[c], 8),
        load(wd_hbm, wd.at[c], 9),
    ]

    barrier = pltpu.get_barrier_semaphore()

    @pl.loop(0, nz - 1)
    def _(i):
        pl.semaphore_signal(barrier, inc=1, device_id=z_peer(i)[1], device_id_type=MESH)

    @pl.loop(0, nt - 1)
    def _(i):
        pl.semaphore_signal(barrier, inc=1, device_id=t_peer(i)[1], device_id_type=MESH)

    pl.semaphore_signal(barrier, inc=1, device_id=sibling, device_id_type=MESH)
    pl.semaphore_wait(barrier, nz + nt - 1)

    def push(source, target, sent, landed, device):
        return pltpu.make_async_remote_copy(
            src_ref=source,
            dst_ref=target,
            send_sem=sent,
            recv_sem=landed,
            device_id=device,
            device_id_type=MESH,
        )

    swaps = [
        push(source, target.at[c], swap_send.at[k], swap_recv.at[k], sibling)
        for k, (source, target) in enumerate(((wo_hbm, wo), (wgu_hbm, wgu), (wd_hbm, wd)))
    ]

    def send(phase, peer_of, count, source, target):
        @pl.loop(0, count - 1)
        def _(i):
            peer, device = peer_of(i)
            push(source(peer), target, send_sem.at[phase], recv_sem.at[phase], device).start()

    def await_bytes(sem, ref):
        pltpu.make_async_copy(ref, ref, sem).wait()

    def block(ref, index):
        return ref.at[pl.ds(pl.multiple_of(index * nt, nt), nt)]

    def first(ref, count):
        return ref.at[pl.ds(0, count)]

    def landed(phase, ref):
        await_bytes(recv_sem.at[phase], ref)

    def sent(phase, ref):
        await_bytes(send_sem.at[phase], ref)

    def send_latent():
        xs = states[...]
        scaled = (xs * ag_ref[...]).astype(BF16)
        a_rows[:, :key_width] = jnp.dot(scaled, wl[...], preferred_element_type=F32)
        squares = jnp.sum(xs * xs, axis=1, keepdims=True)
        a_rows[:, lat + 128 :] = jnp.broadcast_to(squares, (nt, 128))
        for i in range(nt):
            a_send[i] = a_rows[i : i + 1, :]
        a_recv[t] = a_send[t]
        send(0, t_peer, nt, lambda peer: a_send.at[peer], a_recv.at[t])

    a_rows[...] = jnp.zeros_like(a_rows)
    fresh[...] = jnp.zeros_like(fresh)
    latents[...] = jnp.zeros_like(latents)
    b_send[...] = jnp.zeros_like(b_send)
    for one in loads[:3]:
        one.wait()
    states[...] = x_ref[...].astype(F32)
    send_latent()

    length = len_ref[0]
    for one in loads[3:]:
        one.wait()
    row = lax.broadcasted_iota(jnp.int32, turns.shape[1:], 0)
    angles = (row + length).astype(F32) * freq_ref[...]
    turns[0] = jnp.cos(angles)
    turns[1] = jnp.sin(angles)
    mg_inv[...] = 1.0 / mg_ref[...]

    def attend(low, high, arriving):
        rows = pl.ds(low * head_count, (high - low) * head_count)
        queries = q_ref[low:high].reshape((high - low) * head_count, key_width)
        peak[rows, :] = jnp.full((rows.size, 128), -jnp.inf, F32)

        @pl.loop(0, chunks)
        def _(index):
            if arriving:
                load_kv(index).wait()
            place = pl.ds(pl.multiple_of(index * chunk, chunk), chunk)
            part = jnp.dot(queries, kv[:, place], preferred_element_type=F32) * score_scale
            column = lax.broadcasted_iota(jnp.int32, (1, chunk), 1) + index * chunk
            part = jnp.where(column < length, part, -jnp.inf)
            scores[rows, place] = part
            highest = peak[rows, :]
            for k in range(0, chunk, 128):
                highest = jnp.maximum(highest, part[:, k : k + 128])
            peak[rows, :] = highest

        top = jnp.max(peak[rows, :], axis=1, keepdims=True)
        peak[rows, :] = jnp.broadcast_to(top, (rows.size, 128))
        total[rows, :] = jnp.zeros((rows.size, 128), F32)
        old[rows, :] = jnp.zeros((rows.size, lat), F32)

        @pl.loop(0, chunks)
        def _(index):
            place = pl.ds(pl.multiple_of(index * chunk, chunk), chunk)
            weights = jnp.exp(scores[rows, place] - peak[rows, :1])
            running = total[rows, :]
            for k in range(0, chunk, 128):
                running = running + weights[:, k : k + 128]
            total[rows, :] = running
            old[rows, :] += lax.dot_general(
                weights.astype(BF16), kv[:lat, place], NT, preferred_element_type=F32
            )

        sums = jnp.sum(total[rows, :], axis=1, keepdims=True)
        total[rows, :] = jnp.broadcast_to(sums, (rows.size, 128))
        rest = jnp.zeros((128 - head_count, 128), F32)
        for s in range(low, high):
            here = pl.ds(s * head_count, head_count)
            peak_rows[s] = jnp.concatenate([peak[here, :], rest], axis=0).T[:1, :]
            total_rows[s] = jnp.concatenate([total[here, :], rest], axis=0).T[:1, :]

    def head_rows(s):
        start = s * head_count
        return pl.ds(start if isinstance(s, int) else pl.multiple_of(start, head_count), head_count)

    def send_old(s):
        rows = head_rows(s)
        whole = old[rows, :] / total[rows, :1]
        for h in range(head_count):
            o_send[s, h] = whole[h : h + 1, :]
        mine = pl.ds(z * per, per)
        o_recv[s, :, z] = o_send[s, mine]

        @pl.loop(0, nz - 1)
        def _(i):
            peer, device = z_peer(i)
            theirs = pl.ds(peer * per, per)
            push(
                o_send.at[s, theirs], o_recv.at[s, :, z], o_sent.at[s], o_sem.at[s], device
            ).start()

    wide = half_per * lat // 2
    sides = [pl.ds(0, wide), pl.ds(wide, wide)]

    def build_old(s):
        await_bytes(o_sem.at[s], o_send.at[s, pl.ds(0, per * (nz - 1))])
        await_bytes(o_sent.at[s], o_send.at[s, pl.ds(0, per * (nz - 1))])
        for h in range(half_per):
            pair = [o_recv[s, k * half_per + h, :, 0, :] for k in range(2)]
            old_heads[s, t, :, h * lat : (h + 1) * lat] = jnp.concatenate(pair, axis=0).astype(BF16)

    def share_old(s, part):
        @pl.loop(0, nt - 1)
        def _(i):
            piece = old_heads.at[s, t, :, sides[part]]
            push(piece, piece, p_sent.at[2 * s + part], p_sem.at[2 * s + part], t_peer(i)[1]).start()

    def await_old(s, count):
        for part in range(2):
            piece = old_heads.at[s, pl.ds(0, count), :, sides[part]]
            await_bytes(p_sem.at[2 * s + part], piece)
            await_bytes(p_sent.at[2 * s + part], piece)

    def start_keys(s):
        landed(0, first(a_recv, nt - 1))
        sent(0, first(a_send, nt - 1))
        raw = jnp.sum(a_recv[...], axis=0)
        inverse = lax.rsqrt(raw[:, lat + 128 : lat + 129] / width + norm_eps)
        raw = raw * inverse
        content = raw[:, :lat]
        spread = jnp.mean(content * content, axis=1, keepdims=True)
        content = content * lax.rsqrt(spread + norm_eps) * kg_ref[...]
        rope = raw[:, lat : lat + 128]
        half = (key_width - lat) // 2
        lane = lax.broadcasted_iota(jnp.int32, (1, 128), 1)
        turned = jnp.where(
            lane < half, -pltpu.roll(rope, 128 - half, 1), pltpu.roll(rope, half, 1)
        )
        now = pl.ds(s, 1)
        rope = rope * turns[0, now, :] + turned * turns[1, now, :]
        latent = jnp.concatenate([content, rope], axis=1)[:, :key_width].astype(BF16)
        fresh[pl.ds(s, 1), :] = latent.astype(F32)

        keys = fresh[...].astype(BF16)
        recent = lax.dot_general(keys, q_ref[s], NT, preferred_element_type=F32) * score_scale
        place = lax.broadcasted_iota(jnp.int32, recent.shape, 0)
        recent = jnp.where(place <= s, recent, -jnp.inf)
        top_old = peak_rows[s, :, :head_count]
        highest = jnp.maximum(top_old, jnp.max(recent, axis=0, keepdims=True))
        weight_old = total_rows[s, :, :head_count] * jnp.exp(top_old - highest)
        weight_new = jnp.exp(recent - highest)
        denominator = weight_old + jnp.sum(weight_new, axis=0, keepdims=True)
        share_new = (weight_new / denominator).astype(BF16).astype(F32)
        b_send[0, :, :lat] = latent[:, :lat].astype(F32)
        b_send[0, :, lat : lat + head_count] = weight_old / denominator
        for k in range(steps):
            start = lat + (k + 1) * 128
            b_send[0, :, start : start + head_count] = share_new[k : k + 1, :]
        b_recv[z] = b_send[0]
        send(1, z_peer, nz, lambda peer: b_send.at[0], b_recv.at[z])
    def share_keys(s):
        landed(1, first(b_recv, nz - 1))
        sent(1, first(b_recv, nz - 1))
        news = b_recv[:, 0, :]
        lane = lax.broadcasted_iota(jnp.int32, (nz, 128), 1)
        coarse = jnp.zeros((nz, 128), F32)
        for k in range(steps + 1):
            moved = pltpu.roll(
                news[:, lat + k * 128 : lat + (k + 1) * 128],
                lax.rem(k * per - z * per + 128, 128),
                1,
            )
            coarse = jnp.where((lane >= k * per) & (lane < (k + 1) * per), moved, coarse)
        fine = coarse - coarse.astype(BF16).astype(F32)
        upper = jnp.concatenate([news[:, : lat // 2], coarse], axis=1)
        lower = jnp.concatenate([news[:, lat // 2 : lat], fine], axis=1)
        l_all[t] = jnp.concatenate([upper, lower], axis=0).astype(BF16)
        send(2, t_peer, nt, lambda peer: l_all.at[t], l_all.at[t])
    attend(0, 1, True)
    send_old(0)
    start_keys(0)
    for one in own_weights + swaps:
        one.start()
    build_old(0)
    first_hop = ((x_peer, sides[0]), (y_peer, sides[1]))
    for part, (peer_of, cols) in enumerate(first_hop):

        @pl.loop(0, side - 1)
        def _(i, part=part, peer_of=peer_of, cols=cols):
            piece = old_heads.at[0, t, :, cols]
            push(piece, piece, q_sem.at[part], q_sem.at[2 + part], peer_of(i)[1]).start()

    share_keys(0)
    for part, (_, cols) in enumerate(first_hop):
        await_bytes(q_sem.at[2 + part], old_heads.at[0, pl.ds(0, side - 1), :, cols])
        await_bytes(q_sem.at[part], old_heads.at[0, pl.ds(0, side - 1), :, cols])

    @pl.loop(0, side - 1)
    def _(i):
        for j in range(side):
            piece = old_heads.at[0, j * side + yy, :, sides[0]]
            push(piece, piece, p_sent.at[0], p_sem.at[0], y_peer(i)[1]).start()
        piece = old_heads.at[0, pl.ds(xx * side, side), :, sides[1]]
        push(piece, piece, p_sent.at[1], p_sem.at[1], x_peer(i)[1]).start()

    attend(1, steps, False)

    @pl.loop(1, steps)
    def _(s):
        send_old(s)

    for one in own_weights:
        one.wait()
    for one in swaps:
        one.wait()
    for source, target in ((wo, wo_rows), (wd, wd_rows)):
        size = min(256, source.shape[2] // 2)
        while source.shape[2] % size:
            size -= 128
        for k in range(2):

            @pl.loop(0, source.shape[2] // size)
            def _(i):
                place = pl.ds(pl.multiple_of(i * size, size), size)
                target[k, place, :] = source[k, :, place].T
    await_old(0, side * (side - 1))

    @pl.loop(0, steps)
    def _(s):
        landed(2, first(l_all, nt - 1))
        sent(2, first(l_all, nt - 1))

        news = l_all[...].astype(F32)
        upper = news[:, :nz, :].reshape(nt * nz, -1)
        lower = news[:, nz:, :].reshape(nt * nz, -1)
        latents[s] = jnp.concatenate([upper[:, : lat // 2], lower[:, : lat // 2]], axis=1)
        table = upper[:, lat // 2 :] + lower[:, lat // 2 :]
        for h in range(half_per):
            pair = old_heads[s, :, :, h * lat : (h + 1) * lat].astype(F32)
            for k in range(2):
                number = k * half_per + h
                joined = pair[:, k * nz : (k + 1) * nz, :].reshape(nt * nz, lat)
                joined = joined * table[:, number : number + 1]
                for j in range(steps):
                    at = (j + 1) * per + number
                    joined = joined + latents[j] * table[:, at : at + 1]
                heads[k, :, h * lat : (h + 1) * lat] = joined.astype(BF16)

        for part, (low, high) in enumerate(parts):
            cols = pl.ds(low, high - low)
            attended = sum(
                jnp.dot(heads[k], wo_rows[k, :, low:high], preferred_element_type=F32)
                for k in range(2)
            )
            for k in range(low, high, 128):
                size = min(128, high - k)
                y_rows[k // 128, :, :size] = attended[:, k - low : k - low + size]
            for i in range(nz):
                for k in range(low, high, 128):
                    size = min(128, high - k)
                    picked = y_rows[k // 128, pl.ds(i, nt, stride=nz), :]
                    y_send[i, :, k : k + size] = picked[:, :size].astype(BF16)
            y_recv[z, :, cols] = y_send[z, :, cols]
            send(
                3 + part,
                z_peer,
                nz,
                lambda peer, cols=cols: y_send.at[peer, :, cols],
                y_recv.at[z, :, cols],
            )

        @pl.when(s < steps - 1)
        def _():
            build_old(s + 1)
            share_old(s + 1, 0)

        for part, (low, high) in enumerate(parts):
            cols = pl.ds(low, high - low)
            landed(3 + part, y_recv.at[pl.ds(0, nz - 1), :, cols])
            residual = states[:, cols] + jnp.sum(y_recv[:, :, cols].astype(F32), axis=0)
            resid[:, cols] = residual
            mine = normed.at[pl.ds(pl.multiple_of(z * nt, nt), nt), cols]
            mine[...] = (residual * mg_ref[:, cols]).astype(BF16)
            send(5 + part, z_peer, nz, lambda peer, mine=mine: mine, mine)
        for part, (low, high) in enumerate(parts):
            cols = pl.ds(low, high - low)
            landed(5 + part, normed.at[pl.ds(0, nt * (nz - 1)), cols])
            sent(3 + part, y_send.at[pl.ds(0, nz - 1), :, cols])
            sent(5 + part, normed.at[pl.ds(0, nt * (nz - 1)), cols])

        rows = normed[...]
        unscaled = rows.astype(F32) * mg_inv[...]
        squares = jnp.sum(unscaled * unscaled, axis=1, keepdims=True)
        coarse = squares.astype(BF16).astype(F32)
        lane = lax.broadcasted_iota(jnp.int32, (nt * nz, 128), 1)
        pair = jnp.where(lane < 64, coarse, squares - coarse).astype(BF16)
        for i in range(nt):
            here = i // 2 * nt
            gate_send[i // side, i % side, :, :128] = pair[here : here + nt, :]
        halves = ((0, cut), (cut, ff))
        gate_cols = [pl.ds(0, 128 + cut), pl.ds(128 + cut, ff - cut)]
        up_cols = [pl.ds(0, cut), pl.ds(cut, ff - cut)]

        def three(ref, cols):
            return ref.at[pl.ds(0, side - 1), :, :, cols]

        def three_mid(ref, cols):
            return ref.at[pl.ds(0, side - 1), :, cols]

        for part, (low, high) in enumerate(halves):
            cols = gate_cols[part]
            for k in range(2):
                gate = jnp.dot(rows, wgu[k, 0, :, low:high], preferred_element_type=F32)
                gate = gate.astype(BF16)
                for i in range(nz):
                    place = 2 * i + k
                    gate_send[place // side, place % side, :, 128 + low : 128 + high] = gate[
                        i * nt : (i + 1) * nt, :
                    ]
            gate_recv[xx, :, :, cols] = gate_send[xx, :, :, cols]
            send(
                7 + part,
                x_peer,
                side,
                lambda peer, cols=cols: gate_send.at[peer, :, :, cols],
                gate_recv.at[xx, :, :, cols],
            )
            cols = up_cols[part]
            for k in range(2):
                up = jnp.dot(rows, wgu[k, 1, :, low:high], preferred_element_type=F32)
                up = up.astype(BF16)
                for i in range(nz):
                    place = 2 * i + k
                    up_send[place % side, place // side, :, low:high] = up[i * nt : (i + 1) * nt, :]
            up_recv[yy, :, :, cols] = up_send[yy, :, :, cols]
            send(
                9 + part,
                y_peer,
                side,
                lambda peer, cols=cols: up_send.at[peer, :, :, cols],
                up_recv.at[yy, :, :, cols],
            )
        for part in range(2):
            cols = gate_cols[part]
            landed(7 + part, three(gate_recv, cols))
            for i in range(side):
                gate_mid[i, :, cols] = jnp.sum(gate_recv[:, i, :, cols].astype(F32), axis=0).astype(
                    BF16
                )
            gate_last[yy, :, cols] = gate_mid[yy, :, cols]
            send(
                11 + part,
                y_peer,
                side,
                lambda peer, cols=cols: gate_mid.at[peer, :, cols],
                gate_last.at[yy, :, cols],
            )
            cols = up_cols[part]
            landed(9 + part, three(up_recv, cols))
            for i in range(side):
                up_mid[i, :, cols] = jnp.sum(up_recv[:, i, :, cols].astype(F32), axis=0).astype(
                    BF16
                )
            up_last[xx, :, cols] = up_mid[xx, :, cols]
            send(
                13 + part,
                x_peer,
                side,
                lambda peer, cols=cols: up_mid.at[peer, :, cols],
                up_last.at[xx, :, cols],
            )
        place = lax.rem(t, 2) * nz + t // 2
        inverse = None
        for part, (low, high) in enumerate(halves):
            cols = gate_cols[part]
            landed(11 + part, three_mid(gate_last, cols))
            gate = jnp.sum(gate_last[:, :, cols].astype(F32), axis=0)
            if part == 0:
                squares = jnp.sum(gate[:, :128], axis=1, keepdims=True) / 64
                inverse = lax.rsqrt(squares / width + norm_eps)
                gate = gate[:, 128:]
            gate = gate * inverse
            gate = gate * jax.nn.sigmoid(gate) * inverse
            cols = up_cols[part]
            landed(13 + part, three_mid(up_last, cols))
            up = jnp.sum(up_last[:, :, cols].astype(F32), axis=0)
            mine = hidden.at[pl.ds(pl.multiple_of(place * nt, nt), nt), cols]
            mine[...] = (gate * up).astype(BF16)
            send(15 + part, t_peer, nt, lambda peer, mine=mine: mine, mine)
        for part in range(2):
            sent(7 + part, three(gate_send, gate_cols[part]))
            sent(9 + part, three(up_send, up_cols[part]))
            sent(11 + part, three_mid(gate_mid, gate_cols[part]))
            sent(13 + part, three_mid(up_mid, up_cols[part]))

        landed(15, hidden.at[pl.ds(0, nt * (nt - 1)), up_cols[0]])
        half_rows = nz * nt
        early = sum(
            jnp.dot(
                hidden[k * half_rows : (k + 1) * half_rows, :cut],
                wd_rows[k, :cut, :],
                preferred_element_type=F32,
            )
            for k in range(2)
        )
        landed(16, hidden.at[pl.ds(0, nt * (nt - 1)), up_cols[1]])
        for part, (low, high) in enumerate(parts):
            cols = pl.ds(low, high - low)
            down = early[:, low:high] + sum(
                jnp.dot(
                    hidden[k * half_rows : (k + 1) * half_rows, cut:],
                    wd_rows[k, cut:, low:high],
                    preferred_element_type=F32,
                )
                for k in range(2)
            )
            d_send[:, cols] = down.astype(BF16)
            d_recv[z, :, cols] = d_send[pl.ds(pl.multiple_of(z * nt, nt), nt), cols]
            send(
                17 + part,
                z_peer,
                nz,
                lambda peer, cols=cols: d_send.at[
                    pl.ds(pl.multiple_of(peer * nt, nt), nt), cols
                ],
                d_recv.at[z, :, cols],
            )
        @pl.when(s < steps - 1)
        def _():
            share_old(s + 1, 1)

        for part in range(2):
            sent(15 + part, hidden.at[pl.ds(0, nt * (nt - 1)), up_cols[part]])
        for part, (low, high) in enumerate(parts):
            cols = pl.ds(low, high - low)
            landed(17 + part, d_recv.at[pl.ds(0, nz - 1), :, cols])
            sent(17 + part, d_send.at[pl.ds(0, nt * (nz - 1)), cols])
        mixed = (resid[...] + jnp.sum(d_recv[...].astype(F32), axis=0)).astype(BF16)
        out_ref[s] = mixed
        states[...] = mixed.astype(F32)

        @pl.when(s < steps - 1)
        def _():
            send_latent()
            start_keys(s + 1)
            share_keys(s + 1)
            await_old(s + 1, nt - 1)

    lat_out[...] = fresh[:steps, :].astype(BF16)


def hand_out(mixed_ref, lat_ref, mixed_hbm, lat_hbm, sem):
    one = pltpu.make_async_copy(mixed_ref, mixed_hbm, sem.at[0])
    two = pltpu.make_async_copy(lat_ref, lat_hbm, sem.at[1])
    one.start()
    two.start()
    one.wait()
    two.wait()


def body(token_states, queries, kv_cache, lengths, attn_gain, kv_gain, w_latent, w_out, mlp_gain, w_gate_up, w_down):
    nt, width = token_states.shape
    nz = nt // 2
    side = int(round(nt**0.5))
    steps, _, head_count, key_width = queries.shape
    slots = kv_cache.shape[1]
    lat = kv_gain.shape[0]
    ff = w_down.shape[0]
    depth = w_out.shape[0]
    per = head_count // nz
    half = (key_width - lat) // 2
    frequency = np.zeros((1, 128), np.float32)
    frequency[0, : 2 * half] = np.tile(10000.0 ** (-np.arange(half) / half), 2)
    chunk = min(1024, slots)
    rows = steps * head_count
    vmem = pl.BlockSpec(memory_space=pltpu.VMEM)
    hbm = pl.BlockSpec(memory_space=pl.ANY)
    news = lat + (steps + 1) * 128
    block = lat // 2 + 128
    mixed, latents = pl.pallas_call(
        functools.partial(layer_kernel, float(width * lax.axis_size("tp"))),
        out_shape=(
            jax.ShapeDtypeStruct((steps, nt, width), BF16),
            jax.ShapeDtypeStruct((steps, key_width), BF16),
        ),
        in_specs=[hbm, hbm, pl.BlockSpec(memory_space=pltpu.SMEM)] + [hbm] * 9,
        out_specs=(vmem, vmem),
        scratch_shapes=[
            pltpu.VMEM((nt, width), BF16),
            pltpu.VMEM((steps, head_count, key_width), BF16),
            pltpu.VMEM((1, width), F32),
            pltpu.VMEM((1, lat), F32),
            pltpu.VMEM((1, width), F32),
            pltpu.VMEM((1, 128), F32),
            pltpu.VMEM((key_width, slots), BF16),
            pltpu.VMEM(w_latent.shape, BF16),
            pltpu.VMEM((2, width, depth), BF16),
            pltpu.VMEM((2,) + w_gate_up.shape, BF16),
            pltpu.VMEM((2, width, ff), BF16),
            pltpu.VMEM((2, depth, width), BF16),
            pltpu.VMEM((2, ff, width), BF16),
            pltpu.VMEM((2, 8, 128), F32),
            pltpu.VMEM((1, width), F32),
            pltpu.VMEM((rows, slots), F32),
            pltpu.VMEM((rows, 128), F32),
            pltpu.VMEM((rows, 128), F32),
            pltpu.VMEM((steps, 1, 128), F32),
            pltpu.VMEM((steps, 1, 128), F32),
            pltpu.VMEM((rows, lat), F32),
            pltpu.VMEM((nt, width), F32),
            pltpu.VMEM((nt, width), F32),
            pltpu.VMEM((16, key_width), F32),
            pltpu.VMEM((nt, lat + 256), F32),
            pltpu.VMEM((nt, 1, lat + 256), F32),
            pltpu.VMEM((nt, 1, lat + 256), F32),
            pltpu.VMEM((steps, head_count, 1, lat), F32),
            pltpu.VMEM((steps, per, nz, 1, lat), F32),
            pltpu.VMEM((steps, nt, 2 * nz, per // 2 * lat), BF16),
            pltpu.VMEM((1, 1, news), F32),
            pltpu.VMEM((nz, 1, news), F32),
            pltpu.VMEM((nt, 2 * nz, block), BF16),
            pltpu.VMEM((steps, nt * nz, lat), F32),
            pltpu.VMEM((2, nt * nz, depth), BF16),
            pltpu.VMEM((-(-width // 128), nt * nz, 128), F32),
            pltpu.VMEM((nz, nt, width), BF16),
            pltpu.VMEM((nz, nt, width), BF16),
            pltpu.VMEM((nz * nt, width), BF16),
            pltpu.VMEM((side, side, nt, ff + 128), BF16),
            pltpu.VMEM((side, side, nt, ff + 128), BF16),
            pltpu.VMEM((side, nt, ff + 128), BF16),
            pltpu.VMEM((side, nt, ff + 128), BF16),
            pltpu.VMEM((side, side, nt, ff), BF16),
            pltpu.VMEM((side, side, nt, ff), BF16),
            pltpu.VMEM((side, nt, ff), BF16),
            pltpu.VMEM((side, nt, ff), BF16),
            pltpu.VMEM((nt * nt, ff), BF16),
            pltpu.VMEM((nz * nt, width), BF16),
            pltpu.VMEM((nz, nt, width), BF16),
            pltpu.SemaphoreType.DMA((10 + slots // chunk,)),
            pltpu.SemaphoreType.DMA((3,)),
            pltpu.SemaphoreType.DMA((3,)),
            pltpu.SemaphoreType.DMA((19,)),
            pltpu.SemaphoreType.DMA((19,)),
            pltpu.SemaphoreType.DMA((steps,)),
            pltpu.SemaphoreType.DMA((steps,)),
            pltpu.SemaphoreType.DMA((2 * steps,)),
            pltpu.SemaphoreType.DMA((2 * steps,)),
            pltpu.SemaphoreType.DMA((4,)),
        ],
        compiler_params=pltpu.CompilerParams(
            collective_id=0, has_side_effects=True, vmem_limit_bytes=56 * 1024 * 1024
        ),
        name="decode_layer",
    )(
        token_states,
        queries.reshape(steps, head_count, key_width),
        lengths,
        attn_gain.reshape(1, -1),
        kv_gain.reshape(1, -1),
        mlp_gain.reshape(1, -1),
        jnp.asarray(frequency),
        kv_cache.reshape(slots, key_width).T,
        w_latent,
        w_out.T,
        w_gate_up,
        w_down.T,
    )
    return mixed, latents.reshape(steps, 1, key_width)


def solution(mesh):
    placed = (
        P("dp", "tp"),
        P(None, ("dp", "tp"), None, None),
        P(("dp", "tp"), None, None),
        P(("dp", "tp")),
        P("tp"),
        P(),
        P("tp", None),
        P("dp", "tp"),
        P("tp"),
        P(None, "tp", "dp"),
        P("dp", "tp"),
    )
    return jax.shard_map(
        body,
        mesh=mesh,
        in_specs=placed,
        out_specs=(P(None, "dp", "tp"), P(None, ("dp", "tp"), None)),
        check_vma=False,
    )
```
